256 devices in a mesh: row: 8 (over z), col: 16 (over x, y), vox: 2 (over core).
Axes of the slice: x: 4, y: 4, z: 8, core: 2. Of those that a mesh axis runs over, the one named last changes fastest.
Arguments:
- maps: bfloat16 [16384, 2048], P(('row', 'col'), 'vox'), may hold values from -21 to 21
- probes: bfloat16 [16384, 256], P(('row', 'col')), may hold values from -0.046875 to 0.046875
Outputs:
- gram: float32 [16384, 8, 16, 128], P('row', 'vox', 'col')
- basis: float32 [16384, 256], P(('row', 'col', 'vox'))
- factor: float32 [256, 256], replicated
The draws below stay inside these ranges and needn't reach their ends.
All inputs are finite; a program needn't handle non-finite values.
Results may differ from the reference program's by a relative error of at most 0.004.
Values may be sent and summed in bfloat16 or wider, within the bound.
No kernel may reach another device: no remote copies, remote signals or barrier semaphores. Data moves between devices by JAX's collectives and lax.ppermute only.
A program may use at most 64 MiB of HBM per device.

```python
import math
import jax
import jax.numpy as jnp
from jax import lax

SUB_DEV = 128
VOX = 2048
PROBES = 256
SUBJECTS = 16384
ROW_GROUPS = 8
COL_GROUPS = 16


def draw_maps(key, part):
    key = jax.random.fold_in(key, 11)
    keys = jax.random.split(key, 5)
    base = jax.random.uniform(keys[0], (1, VOX), jnp.float32, -4.0, 4.0)
    trend = jnp.clip(jax.random.normal(keys[1], (1, VOX), jnp.float32), -4.0, 4.0)
    position = jnp.arange(SUBJECTS, dtype=jnp.float32)[:, None] / (SUBJECTS - 1)
    spread = jnp.exp(jax.random.uniform(keys[2], (SUBJECTS, 1), jnp.float32, math.log(0.7), math.log(1.4)))
    scale = (1.0 + 2.0 * position) * spread
    load = 0.1 * (0.5 + position) * jax.random.uniform(keys[3], (SUBJECTS, 1), jnp.float32, 0.8, 1.2)
    noise = jnp.clip(jax.random.normal(keys[4], (SUBJECTS, VOX), jnp.float32), -3.5, 3.5)
    return (base + load * trend + scale * noise).astype(jnp.bfloat16)


def block_levels(key, extent, cuts, least, high):
    def one(dim, blocks):
        draws = jax.random.uniform(jax.random.fold_in(jax.random.fold_in(key, 6), dim), (blocks,), jnp.float32, least / len(cuts), high / len(cuts))
        return jnp.repeat(jnp.exp(draws), extent[dim] // blocks).reshape((-1,) + (1,) * (len(extent) - dim - 1))

    level = one(*cuts[0])
    for cut in cuts[1:]:
        level = level * one(*cut)
    return level


def centred(key, extent, scale, bound, cuts=(), kind=jnp.bfloat16):
    drawn = scale * jax.random.normal(key, extent, jnp.float32)
    if cuts:
        drawn = drawn * block_levels(key, extent, cuts, -0.22, 0.18)
    return jnp.clip(drawn, -bound, bound).astype(kind)


def setup_inputs(seed: int = 0) -> dict:
    arg_keys = jax.random.split(jax.random.key(seed), 3)
    maps = draw_maps(jax.random.fold_in(arg_keys[2], 71), 0)
    probes = centred(arg_keys[1], (SUBJECTS, PROBES), SUBJECTS ** -0.5, 0.046875, ((0, 128),))
    return {"maps": maps, "probes": probes}


def reference(maps, probes):
    flat = maps.astype(jnp.float32)
    voxel_mean = jnp.sum(flat, axis=0) / SUBJECTS
    centered = (flat - voxel_mean[None, :]).astype(jnp.bfloat16)
    kernel = jnp.dot(centered.astype(jnp.float32), centered.T.astype(jnp.float32), preferred_element_type=jnp.float32) / VOX
    sketch = jnp.dot(kernel, probes.astype(jnp.float32), precision=lax.Precision.HIGHEST)
    cross = lax.dot_general(sketch, sketch, (((0,), (0,)), ((), ())), precision=lax.Precision.HIGHEST) / SUBJECTS
    lower = jnp.linalg.cholesky(cross)
    basis = jax.scipy.linalg.solve_triangular(lower, sketch.T, lower=True).T
    gram = kernel.reshape(SUBJECTS, ROW_GROUPS, COL_GROUPS, SUB_DEV)
    return (gram, basis, lower.T)
```

```python
import functools

import jax
import jax.numpy as jnp
from jax import lax
from jax.experimental import pallas as pl
from jax.experimental.pallas import tpu as pltpu
from jax.sharding import PartitionSpec as P

F32 = jnp.float32
BF16 = jnp.bfloat16
HIGHEST = lax.Precision.HIGHEST
PAD = 8
PARAMS = pltpu.CompilerParams(vmem_limit_bytes=48 * 1024 * 1024)


def call(kernel, out_shape, *args, **kw):
    return pl.pallas_call(kernel, out_shape=out_shape, compiler_params=PARAMS, **kw)(*args)


def sd(shape, dtype=F32):
    return jax.ShapeDtypeStruct(shape, dtype)


def project_kernel(pieces, maps_ref, probes_ref, out_ref):
    maps = maps_ref[...]
    probes = probes_ref[...]
    vox, cols = maps.shape[1], probes.shape[1]
    width = vox // pieces
    sums = jnp.sum(maps.astype(F32), axis=0, keepdims=True)
    probe_sums = jnp.sum(probes.astype(F32), axis=0, keepdims=True)
    product = lax.dot_general(maps, probes, (((0,), (0,)), ((), ())), preferred_element_type=F32)
    for k in range(pieces):
        base = k * (width + PAD)
        out_ref[base : base + width, :] = product[k * width : (k + 1) * width, :]
        out_ref[base + width : base + width + 1, :width] = sums[:, k * width : (k + 1) * width]
        out_ref[base + width + 1 : base + width + 2, :] = probe_sums


def sum_repeat_kernel(sources, copies, in_ref, out_ref):
    rows = in_ref.shape[0] // sources
    total = in_ref[0:rows, :]
    for k in range(1, sources):
        total = total + in_ref[k * rows : (k + 1) * rows, :]
    for k in range(copies):
        out_ref[k * rows : (k + 1) * rows, :] = total


def centre_kernel(sources, copies, subjects, in_ref, out_ref):
    rows = in_ref.shape[0] // sources
    width = rows - PAD
    total = in_ref[0:rows, :]
    for k in range(1, sources):
        total = total + in_ref[k * rows : (k + 1) * rows, :]
    mean = total[width : width + 1, :width] / subjects
    probe_sums = total[width + 1 : width + 2, :]
    square = (width, width)
    on_diagonal = lax.broadcasted_iota(jnp.int32, square, 0) == lax.broadcasted_iota(
        jnp.int32, square, 1
    )
    mean_column = jnp.sum(jnp.where(on_diagonal, mean, 0.0), axis=1, keepdims=True)
    piece = total[:width, :] - mean_column * probe_sums
    for k in range(copies):
        out_ref[k * rows : k * rows + width, :] = piece
        out_ref[k * rows + width : k * rows + width + 1, :width] = mean


def sketch_kernel(pieces, vox_total, pos_ref, maps_ref, w_ref, out_ref, mean_ref, parts):
    rows = w_ref.shape[0] // pieces
    width = rows - PAD

    @pl.when(pl.program_id(0) == 0)
    def _():
        for k in range(pieces):
            w = w_ref[k * rows : k * rows + width, :] * (1.0 / vox_total)
            for n in range(3):
                part = w.astype(BF16)
                parts[n, k * width : (k + 1) * width, :] = part
                w = w - part.astype(F32)
        mean_ref[...] = jnp.concatenate(
            [w_ref[k * rows + width : k * rows + width + 1, :width] for k in range(pieces)], axis=1
        )

    centered = (maps_ref[...].astype(F32) - mean_ref[...]).astype(BF16)
    total = jnp.dot(centered, parts[0], preferred_element_type=F32)
    total += jnp.dot(centered, parts[1], preferred_element_type=F32)
    total += jnp.dot(centered, parts[2], preferred_element_type=F32)
    count, half = out_ref.shape[1], out_ref.shape[2]
    split = total.reshape(count, 2, half, total.shape[1])
    own = pos_ref[0]
    out_ref[own] = split[:, 0]
    out_ref[1 - own] = split[:, 1]


def cross_kernel(subjects, copies, pos_ref, both_ref, got_ref, out_ref, own_ref, full):
    sketch = both_ref[0] + got_ref[...]
    groups, half, cols = sketch.shape
    flat = sketch.reshape(groups * half, cols)
    full[...] = lax.dot_general(
        flat, flat, (((0,), (0,)), ((), ())), precision=HIGHEST, preferred_element_type=F32
    ) * (1.0 / subjects)
    col = pos_ref[1]
    rows = out_ref.shape[0] // copies
    piece = full[pl.ds(pl.multiple_of(col * rows, rows), rows), :]
    for k in range(copies):
        out_ref[k * rows : (k + 1) * rows, :] = piece
    own_ref[...] = both_ref[0, col] + got_ref[col]


def cholesky_kernel(block, cross_ref, own_ref, factor_ref, basis_ref, work):
    size = cross_ref.shape[0]
    mine = own_ref.shape[0]
    work[:, :size] = cross_ref[...]
    padded = jnp.concatenate([own_ref[...], jnp.zeros((128 - mine, size), F32)], axis=0)
    work[:, size:] = padded.T
    below = lax.broadcasted_iota(jnp.int32, (block, 1), 0)
    for start in range(0, size, block):
        lane0 = start // 128 * 128
        panel = work[start : start + block, lane0:]
        scale = jnp.zeros((block, 1), F32)
        for i in range(block):
            lane = start + i - lane0
            column = panel[:, lane : lane + 1]
            pivot = column[i : i + 1, :]
            scale = jnp.where(below == i, lax.rsqrt(pivot), scale)
            if i < block - 1:
                weight = jnp.where(below > i, column * (1.0 / pivot), 0.0)
                panel = panel - weight * panel[i : i + 1, :]
        panel = panel * scale
        work[start : start + block, lane0:] = panel
        stop = start + block
        if stop < size:
            lane1 = stop // 128 * 128
            right = panel[:, lane1 - lane0 :]
            left = panel[:, lane1 - lane0 : size - lane0]
            update = lax.dot_general(
                left, right, (((0,), (0,)), ((), ())), precision=HIGHEST, preferred_element_type=F32
            )
            work[stop:, lane1:] = work[stop:, lane1:] - update[stop - lane1 :, :]
    square = (size, size)
    upper = lax.broadcasted_iota(jnp.int32, square, 0) <= lax.broadcasted_iota(jnp.int32, square, 1)
    factor_ref[...] = jnp.where(upper, work[:, :size], 0.0)
    basis_ref[...] = work[:, size:].T[:mine, :]


def gram_kernel(vox_total, own_ref, other_ref, col_own_ref, col_other_ref, mean_ref, out_ref, cols):
    half = own_ref.shape[1]

    def centre(value, k):
        return (value.astype(F32) - mean_ref[k : k + 1, :]).astype(BF16)

    @pl.when(pl.program_id(0) == 0)
    def _():
        cols[:, :half] = centre(col_own_ref[...], 0)
        cols[:, half:] = centre(col_other_ref[...], 1)

    contract = (((1,), (1,)), ((), ()))
    tile = lax.dot_general(
        centre(own_ref[...], 0), cols[:, :half], contract, preferred_element_type=F32
    )
    tile += lax.dot_general(
        centre(other_ref[...], 1), cols[:, half:], contract, preferred_element_type=F32
    )
    tile = tile * (1.0 / vox_total)
    rows = tile.shape[0]
    groups = tile.shape[1] // 128
    for a in range(groups):
        out_ref[pl.ds(a, rows, stride=groups), :] = tile[:, a * 128 : (a + 1) * 128]


def shards(maps, probes):
    sub_rows, vox_half = maps.shape
    width = probes.shape[1]
    row_count = lax.axis_size("row")
    col_count = lax.axis_size("col")
    vox_count = lax.axis_size("vox")
    subjects = sub_rows * row_count * col_count
    vox_total = vox_half * vox_count
    block_rows = sub_rows * col_count
    groups = row_count // vox_count
    col_pos = lax.axis_index("col")
    vox_pos = lax.axis_index("vox")
    pos = jnp.stack([vox_pos, col_pos]).astype(jnp.int32)
    swap = [(0, 1), (1, 0)]

    def exchange(value, axis):
        return lax.all_to_all(value, axis, 0, 0, tiled=True)

    row_maps = lax.all_gather(maps, "col", axis=0, tiled=True)
    col_maps = lax.all_gather(maps, "row", axis=0, tiled=True)

    slice_rows = vox_half // col_count + PAD
    local = call(
        functools.partial(project_kernel, col_count),
        sd((col_count * slice_rows, width)),
        maps,
        probes,
    )
    part = call(
        functools.partial(sum_repeat_kernel, col_count, row_count),
        sd((row_count * slice_rows, width)),
        exchange(local, "col"),
    )
    whole = call(
        functools.partial(centre_kernel, row_count, col_count, subjects),
        sd((col_count * slice_rows, width)),
        exchange(part, "row"),
    )
    weights = exchange(whole, "col")

    half_rows = sub_rows // vox_count
    step = 2 * sub_rows
    count = step // sub_rows
    both, mean = pl.pallas_call(
        functools.partial(sketch_kernel, col_count, vox_total),
        grid_spec=pltpu.PrefetchScalarGridSpec(
            num_scalar_prefetch=1,
            grid=(block_rows // step,),
            in_specs=[
                pl.BlockSpec((step, vox_half), lambda i, p: (i, 0)),
                pl.BlockSpec((col_count * slice_rows, width), lambda i, p: (0, 0)),
            ],
            out_specs=[
                pl.BlockSpec((2, count, half_rows, width), lambda i, p: (0, i, 0, 0)),
                pl.BlockSpec((1, vox_half), lambda i, p: (0, 0)),
            ],
            scratch_shapes=[pltpu.VMEM((3, vox_half, width), BF16)],
        ),
        out_shape=[sd((2, col_count, half_rows, width)), sd((1, vox_half))],
        compiler_params=PARAMS,
    )(pos, row_maps, weights)
    got = lax.ppermute(both[1], "vox", swap)
    cross_rows = width // col_count
    copies = row_count * vox_count
    slices, own = pl.pallas_call(
        functools.partial(cross_kernel, subjects, copies),
        grid_spec=pltpu.PrefetchScalarGridSpec(
            num_scalar_prefetch=1,
            grid=(1,),
            in_specs=[
                pl.BlockSpec((1, col_count, half_rows, width), lambda i, p: (0, 0, 0, 0)),
                pl.BlockSpec((col_count, half_rows, width), lambda i, p: (0, 0, 0)),
            ],
            out_specs=[
                pl.BlockSpec((copies * cross_rows, width), lambda i, p: (0, 0)),
                pl.BlockSpec((half_rows, width), lambda i, p: (0, 0)),
            ],
            scratch_shapes=[pltpu.VMEM((width, width), F32)],
        ),
        out_shape=[sd((copies * cross_rows, width)), sd((half_rows, width))],
        compiler_params=PARAMS,
    )(pos, both, got)
    summed = call(
        functools.partial(sum_repeat_kernel, copies, col_count),
        sd((width, width)),
        exchange(slices, ("row", "vox")),
    )
    cross = exchange(summed, "col")
    factor, basis = call(
        functools.partial(cholesky_kernel, 32),
        [sd((width, width)), sd((half_rows, width))],
        cross,
        own,
        scratch_shapes=[pltpu.VMEM((width, width + 128), F32)],
    )

    own_cols = groups * sub_rows
    other_rows = lax.ppermute(row_maps, "vox", swap)
    col_own = lax.dynamic_slice_in_dim(col_maps, vox_pos * own_cols, own_cols, 0)
    col_sent = lax.dynamic_slice_in_dim(col_maps, (1 - vox_pos) * own_cols, own_cols, 0)
    col_other = lax.ppermute(col_sent, "vox", swap)
    means = jnp.concatenate([mean, lax.ppermute(mean, "vox", swap)], axis=0)
    tall = 256
    gram = pl.pallas_call(
        functools.partial(gram_kernel, vox_total),
        grid=(block_rows // tall,),
        in_specs=[
            pl.BlockSpec((tall, vox_half), lambda i: (i, 0)),
            pl.BlockSpec((tall, vox_half), lambda i: (i, 0)),
            pl.BlockSpec((own_cols, vox_half), lambda i: (0, 0)),
            pl.BlockSpec((own_cols, vox_half), lambda i: (0, 0)),
            pl.BlockSpec((2, vox_half), lambda i: (0, 0)),
        ],
        out_specs=pl.BlockSpec((tall * groups, 128), lambda i: (i, 0)),
        out_shape=sd((block_rows * groups, 128)),
        scratch_shapes=[pltpu.VMEM((own_cols, vox_total), BF16)],
        compiler_params=PARAMS,
    )(row_maps, other_rows, col_own, col_other, means)
    return gram.reshape(block_rows, groups, 1, sub_rows), basis, factor


def solution(mesh):
    placed = (P(("row", "col"), "vox"), P(("row", "col"), None))
    return jax.shard_map(
        shards,
        mesh=mesh,
        in_specs=placed,
        out_specs=(P("row", "vox", "col", None), P(("row", "col", "vox"), None), P()),
        check_vma=False,
    )
```

```python
import functools

import jax
import jax.numpy as jnp
from jax import lax
from jax.experimental import pallas as pl
from jax.experimental.pallas import tpu as pltpu
from jax.sharding import PartitionSpec as P

F32 = jnp.float32
BF16 = jnp.bfloat16
HIGHEST = lax.Precision.HIGHEST
PAD = 8
PARAMS = pltpu.CompilerParams(vmem_limit_bytes=24 * 1024 * 1024)
LARGE = pltpu.CompilerParams(vmem_limit_bytes=48 * 1024 * 1024)


def call(kernel, out_shape, *args, after=(), **kw):
    count = len(args)

    def body(*refs):
        kernel(*refs[:count], *refs[count + len(after) :])

    specs = [pl.BlockSpec(memory_space=pltpu.VMEM)] * count
    specs += [pl.BlockSpec(memory_space=pl.ANY)] * len(after)
    return pl.pallas_call(
        body, out_shape=out_shape, in_specs=specs, compiler_params=PARAMS, **kw
    )(*args, *after)


def sd(shape, dtype=F32):
    return jax.ShapeDtypeStruct(shape, dtype)


def project_kernel(pieces, maps_ref, probes_ref, out_ref):
    maps = maps_ref[...]
    probes = probes_ref[...]
    vox, cols = maps.shape[1], probes.shape[1]
    width = vox // pieces
    sums = jnp.sum(maps.astype(F32), axis=0, keepdims=True)
    probe_sums = jnp.sum(probes.astype(F32), axis=0, keepdims=True)
    product = lax.dot_general(maps, probes, (((0,), (0,)), ((), ())), preferred_element_type=F32)
    for k in range(pieces):
        base = k * (width + PAD)
        out_ref[base : base + width, :] = product[k * width : (k + 1) * width, :]
        out_ref[base + width : base + width + 1, :width] = sums[:, k * width : (k + 1) * width]
        out_ref[base + width + 1 : base + width + 2, :] = probe_sums


def sum_repeat_kernel(sources, copies, in_ref, out_ref):
    rows = in_ref.shape[0] // sources
    total = in_ref[0:rows, :]
    for k in range(1, sources):
        total = total + in_ref[k * rows : (k + 1) * rows, :]
    for k in range(copies):
        out_ref[k * rows : (k + 1) * rows, :] = total


def centre_kernel(sources, copies, subjects, in_ref, out_ref):
    rows = in_ref.shape[0] // sources
    width = rows - PAD
    total = in_ref[0:rows, :]
    for k in range(1, sources):
        total = total + in_ref[k * rows : (k + 1) * rows, :]
    mean = total[width : width + 1, :width] / subjects
    probe_sums = total[width + 1 : width + 2, :]
    square = (width, width)
    on_diagonal = lax.broadcasted_iota(jnp.int32, square, 0) == lax.broadcasted_iota(
        jnp.int32, square, 1
    )
    mean_column = jnp.sum(jnp.where(on_diagonal, mean, 0.0), axis=1, keepdims=True)
    piece = total[:width, :] - mean_column * probe_sums
    for k in range(copies):
        out_ref[k * rows : k * rows + width, :] = piece
        out_ref[k * rows + width : k * rows + width + 1, :width] = mean


def split_terms(value):
    terms = []
    for _ in range(3):
        term = value.astype(BF16)
        terms.append(term)
        value = value - term.astype(F32)
    return terms


def sketch_kernel(
    pieces, vox_total, pos_ref, maps_ref, w_ref, _, kept_ref, sent_ref, mean_ref, centered_ref, parts
):
    rows = w_ref.shape[0] // pieces
    width = rows - PAD

    @pl.when(pl.program_id(0) == 0)
    def _():
        for k in range(pieces):
            w = w_ref[k * rows : k * rows + width, :] * (1.0 / vox_total)
            for n, part in enumerate(split_terms(w)):
                parts[n, k * width : (k + 1) * width, :] = part
        mean_ref[...] = jnp.concatenate(
            [w_ref[k * rows + width : k * rows + width + 1, :width] for k in range(pieces)], axis=1
        )

    centered = (maps_ref[...].astype(F32) - mean_ref[...]).astype(BF16)
    centered_ref[...] = centered
    total = jnp.dot(centered, parts[0], preferred_element_type=F32)
    total += jnp.dot(centered, parts[1], preferred_element_type=F32)
    total += jnp.dot(centered, parts[2], preferred_element_type=F32)
    count, half = kept_ref.shape[0], kept_ref.shape[1]
    split = total.reshape(count, 2, half, total.shape[1])

    @pl.when(pos_ref[0] == 0)
    def _():
        kept_ref[...] = split[:, 0]
        sent_ref[...] = split[:, 1]

    @pl.when(pos_ref[0] == 1)
    def _():
        kept_ref[...] = split[:, 1]
        sent_ref[...] = split[:, 0]


def sort_kernel(shifts, pos_ref, *refs):
    pieces, kept_ref, sent_ref = refs[:-2], refs[-2], refs[-1]
    groups = kept_ref.shape[0]
    total = 2 * groups
    for (shift, start), piece in zip(shifts, pieces):
        group = lax.rem(pos_ref[2] + (shift + total), total)
        mine = group // groups == pos_ref[0]
        place = lax.rem(group, groups)
        stop = start + piece.shape[0]

        @pl.when(mine)
        def _(piece=piece, place=place, start=start, stop=stop):
            kept_ref[place, start:stop, :] = piece[...]

        @pl.when(jnp.logical_not(mine))
        def _(piece=piece, place=place, start=start, stop=stop):
            sent_ref[place, start:stop, :] = piece[...]


def cross_kernel(subjects, copies, pos_ref, kept_ref, got_ref, _, out_ref, own_ref, __, full):
    sketch = kept_ref[...] + got_ref[...]
    groups, half, cols = sketch.shape
    flat = sketch.reshape(groups * half, cols)
    full[...] = lax.dot_general(
        flat, flat, (((0,), (0,)), ((), ())), precision=HIGHEST, preferred_element_type=F32
    ) * (1.0 / subjects)
    col = pos_ref[1]
    rows = out_ref.shape[0] // copies
    piece = full[pl.ds(pl.multiple_of(col * rows, rows), rows), :]
    for k in range(copies):
        out_ref[k * rows : (k + 1) * rows, :] = piece
    own_ref[...] = kept_ref[col] + got_ref[col]


def cholesky_kernel(block, cross_ref, own_ref, factor_ref, basis_ref, work):
    size = cross_ref.shape[0]
    mine = own_ref.shape[0]
    work[:, :size] = cross_ref[...]
    padded = jnp.concatenate([own_ref[...], jnp.zeros((128 - mine, size), F32)], axis=0)
    work[:, size:] = padded.T
    shape = (block, 128)
    row_id = lax.broadcasted_iota(jnp.int32, shape, 0)

    def spread(value):
        return jnp.broadcast_to(value, shape)

    for start in range(0, size, block):
        lane0 = start // 128 * 128
        chunks = [work[start : start + block, k : k + 128] for k in range(lane0, size + 128, 128)]
        first = start - lane0
        columns = [spread(chunks[0][:, first + j : first + j + 1]) for j in range(block)]
        scale = jnp.zeros(shape, F32)
        for i in range(block):
            pivot = spread(columns[i][i : i + 1, :])
            scale = jnp.where(row_id == i, lax.rsqrt(pivot), scale)
            if i < block - 1:
                weight = jnp.where(row_id > i, columns[i] * (1.0 / pivot), 0.0)
                for j in range(i + 1, block):
                    columns[j] = columns[j] - weight * spread(columns[j][i : i + 1, :])
                chunks = [c - weight * spread(c[i : i + 1, :]) for c in chunks]
        panel = jnp.concatenate([c * scale for c in chunks], axis=1)
        work[start : start + block, lane0:] = panel
        stop = start + block
        if stop < size:
            lane1 = stop // 128 * 128
            right = split_terms(panel[:, lane1 - lane0 :])
            left = [part[:, : size - lane1] for part in right]
            update = lax.dot_general(
                jnp.concatenate([left[k] for k in (0, 0, 1, 0, 2, 1)], axis=0),
                jnp.concatenate([right[k] for k in (0, 1, 0, 2, 0, 1)], axis=0),
                (((0,), (0,)), ((), ())),
                preferred_element_type=F32,
            )
            work[stop:, lane1:] = work[stop:, lane1:] - update[stop - lane1 :, :]
    square = (size, size)
    upper = lax.broadcasted_iota(jnp.int32, square, 0) <= lax.broadcasted_iota(jnp.int32, square, 1)
    factor_ref[...] = jnp.where(upper, work[:, :size], 0.0)
    basis_ref[...] = work[:, size:].T[:mine, :]


def gram_kernel(vox_total, own_ref, other_ref, col_own_ref, col_other_ref, means_ref, out_ref, done_ref, cols):
    half = own_ref.shape[1]

    @pl.when(pl.program_id(0) == 0)
    def _():
        for k, ref in enumerate((col_own_ref, col_other_ref)):
            mean = means_ref[k : k + 1, :]
            cols[:, k * half : (k + 1) * half] = (ref[...].astype(F32) - mean).astype(BF16)

    contract = (((1,), (1,)), ((), ()))
    tile = lax.dot_general(own_ref[...], cols[:, :half], contract, preferred_element_type=F32)
    tile += lax.dot_general(other_ref[...], cols[:, half:], contract, preferred_element_type=F32)
    tile = tile * (1.0 / vox_total)
    done_ref[...] = jnp.zeros(done_ref.shape, F32)
    rows = tile.shape[0]
    groups = tile.shape[1] // 128
    for a in range(groups):
        out_ref[pl.ds(a, rows, stride=groups), :] = tile[:, a * 128 : (a + 1) * 128]


def ring_gather(block, axis, size):
    ahead = [(i, (i + 1) % size) for i in range(size)]
    back = [(i, (i - 1) % size) for i in range(size)]
    found = [((0, 0), block)]
    up = down = block
    half = block.shape[0] // 2
    for k in range(1, size // 2):
        up = lax.ppermute(up, axis, ahead)
        down = lax.ppermute(down, axis, back)
        found += [((-k, 0), up), ((k, 0), down)]
    far = size // 2
    found += [((-far, 0), lax.ppermute(up[:half], axis, ahead))]
    found += [((far, half), lax.ppermute(down[half:], axis, back))]
    return found


def shards(maps, probes):
    sub_rows, vox_half = maps.shape
    width = probes.shape[1]
    row_count = lax.axis_size("row")
    col_count = lax.axis_size("col")
    vox_count = lax.axis_size("vox")
    subjects = sub_rows * row_count * col_count
    vox_total = vox_half * vox_count
    block_rows = sub_rows * col_count
    groups = row_count // vox_count
    col_pos = lax.axis_index("col")
    vox_pos = lax.axis_index("vox")
    pos = jnp.stack([vox_pos, col_pos, lax.axis_index("row")]).astype(jnp.int32)
    swap = [(0, 1), (1, 0)]

    def exchange(value, axis):
        return lax.all_to_all(value, axis, 0, 0, tiled=True)

    row_maps = lax.all_gather(maps, "col", axis=0, tiled=True)
    ring = ring_gather(maps, "row", row_count)
    group_shape = (groups, sub_rows, vox_half)
    whole_block = pl.BlockSpec(group_shape, lambda i, p: (0, 0, 0))
    col_kept, col_sent = pl.pallas_call(
        functools.partial(sort_kernel, [key for key, _ in ring]),
        grid_spec=pltpu.PrefetchScalarGridSpec(
            num_scalar_prefetch=1,
            grid=(1,),
            in_specs=[pl.BlockSpec(piece.shape, lambda i, p: (0, 0)) for _, piece in ring],
            out_specs=[whole_block, whole_block],
        ),
        out_shape=[sd(group_shape, BF16)] * 2,
        compiler_params=PARAMS,
    )(pos, *[piece for _, piece in ring])
    col_other = lax.ppermute(col_sent, "vox", swap)

    slice_rows = vox_half // col_count + PAD
    local = call(
        functools.partial(project_kernel, col_count),
        sd((col_count * slice_rows, width)),
        maps,
        probes,
    )
    part = call(
        functools.partial(sum_repeat_kernel, col_count, row_count),
        sd((row_count * slice_rows, width)),
        exchange(local, "col"),
        after=[piece for _, piece in ring[1:5]],
    )
    whole = call(
        functools.partial(centre_kernel, row_count, col_count, subjects),
        sd((col_count * slice_rows, width)),
        exchange(part, "row"),
    )
    weights = exchange(whole, "col")

    half_rows = sub_rows // vox_count
    step = 4 * sub_rows
    half_spec = pl.BlockSpec((step // sub_rows, half_rows, width), lambda i, p: (i, 0, 0))
    kept, sent, mean, centered = pl.pallas_call(
        functools.partial(sketch_kernel, col_count, vox_total),
        grid_spec=pltpu.PrefetchScalarGridSpec(
            num_scalar_prefetch=1,
            grid=(block_rows // step,),
            in_specs=[
                pl.BlockSpec((step, vox_half), lambda i, p: (i, 0)),
                pl.BlockSpec((col_count * slice_rows, width), lambda i, p: (0, 0)),
                pl.BlockSpec(memory_space=pl.ANY),
            ],
            out_specs=[
                half_spec,
                half_spec,
                pl.BlockSpec((1, vox_half), lambda i, p: (0, 0)),
                pl.BlockSpec((step, vox_half), lambda i, p: (i, 0)),
            ],
            scratch_shapes=[pltpu.VMEM((3, vox_half, width), BF16)],
        ),
        out_shape=[
            sd((col_count, half_rows, width)),
            sd((col_count, half_rows, width)),
            sd((1, vox_half)),
            sd((block_rows, vox_half), BF16),
        ],
        compiler_params=LARGE,
    )(pos, row_maps, weights, col_other)
    got = lax.ppermute(sent, "vox", swap)
    cross_rows = width // col_count
    copies = row_count * vox_count
    slices, own, centered = pl.pallas_call(
        functools.partial(cross_kernel, subjects, copies),
        grid_spec=pltpu.PrefetchScalarGridSpec(
            num_scalar_prefetch=1,
            grid=(1,),
            in_specs=[
                pl.BlockSpec((col_count, half_rows, width), lambda i, p: (0, 0, 0)),
                pl.BlockSpec((col_count, half_rows, width), lambda i, p: (0, 0, 0)),
                pl.BlockSpec(memory_space=pl.ANY),
            ],
            out_specs=[
                pl.BlockSpec((copies * cross_rows, width), lambda i, p: (0, 0)),
                pl.BlockSpec((half_rows, width), lambda i, p: (0, 0)),
                pl.BlockSpec(memory_space=pl.ANY),
            ],
            scratch_shapes=[pltpu.VMEM((width, width), F32)],
        ),
        out_shape=[
            sd((copies * cross_rows, width)),
            sd((half_rows, width)),
            sd((block_rows, vox_half), BF16),
        ],
        input_output_aliases={3: 2},
        compiler_params=PARAMS,
    )(pos, kept, got, centered)
    summed = call(
        functools.partial(sum_repeat_kernel, copies, col_count),
        sd((width, width)),
        exchange(slices, ("row", "vox")),
    )
    cross = exchange(summed, "col")
    other = lax.ppermute(centered, "vox", swap)
    means = jnp.concatenate([mean, lax.ppermute(mean, "vox", swap)], axis=0)
    own_cols = groups * sub_rows
    tall = 256
    gram, done = pl.pallas_call(
        functools.partial(gram_kernel, vox_total),
        grid=(block_rows // tall,),
        in_specs=[
            pl.BlockSpec((tall, vox_half), lambda i: (i, 0)),
            pl.BlockSpec((tall, vox_half), lambda i: (i, 0)),
            pl.BlockSpec((own_cols, vox_half), lambda i: (0, 0)),
            pl.BlockSpec((own_cols, vox_half), lambda i: (0, 0)),
            pl.BlockSpec((2, vox_half), lambda i: (0, 0)),
        ],
        out_specs=[
            pl.BlockSpec((tall * groups, 128), lambda i: (i, 0)),
            pl.BlockSpec((8, 128), lambda i: (0, 0)),
        ],
        out_shape=[sd((block_rows * groups, 128)), sd((8, 128))],
        scratch_shapes=[pltpu.VMEM((own_cols, vox_total), BF16)],
        compiler_params=PARAMS,
    )(
        centered,
        other,
        col_kept.reshape(own_cols, vox_half),
        col_other.reshape(own_cols, vox_half),
        means,
    )
    factor, basis = call(
        functools.partial(cholesky_kernel, 16),
        [sd((width, width)), sd((half_rows, width))],
        cross,
        own,
        after=[done],
        scratch_shapes=[pltpu.VMEM((width, width + 128), F32)],
    )
    return gram.reshape(block_rows, groups, 1, sub_rows), basis, factor


def solution(mesh):
    placed = (P(("row", "col"), "vox"), P(("row", "col"), None))
    return jax.shard_map(
        shards,
        mesh=mesh,
        in_specs=placed,
        out_specs=(P("row", "vox", "col", None), P(("row", "col", "vox"), None), P()),
        check_vma=False,
    )
```

```python
import functools

import jax
import jax.numpy as jnp
from jax import lax
from jax.experimental import pallas as pl
from jax.experimental.pallas import tpu as pltpu
from jax.sharding import PartitionSpec as P

F32 = jnp.float32
BF16 = jnp.bfloat16
HIGHEST = lax.Precision.HIGHEST
PAD = 8
PARAMS = pltpu.CompilerParams(vmem_limit_bytes=24 * 1024 * 1024)
LARGE = pltpu.CompilerParams(vmem_limit_bytes=48 * 1024 * 1024)
ALL = pltpu.CompilerParams(vmem_limit_bytes=58 * 1024 * 1024)


def call(kernel, out_shape, *args, after=(), carry=(), params=PARAMS, **kw):
    count, outs = len(args), len(out_shape)
    others = len(after) + len(carry)

    def body(*refs):
        kernel(*refs[:count], *refs[count + others :][:outs], *refs[count + others + outs + len(carry) :])

    anywhere = pl.BlockSpec(memory_space=pl.ANY)
    vmem = pl.BlockSpec(memory_space=pltpu.VMEM)
    return pl.pallas_call(
        body,
        out_shape=[*out_shape, *[sd(x.shape, x.dtype) for x in carry]],
        in_specs=kw.pop("in_specs", [vmem] * count) + [anywhere] * others,
        out_specs=[vmem] * outs + [anywhere] * len(carry),
        input_output_aliases={count + len(after) + k: outs + k for k in range(len(carry))},
        compiler_params=params,
        **kw,
    )(*args, *after, *carry)


def sd(shape, dtype=F32):
    return jax.ShapeDtypeStruct(shape, dtype)


def project_kernel(pieces, maps_ref, probes_ref, out_ref, maps_in, probes_in, arrived):
    copies = [
        pltpu.make_async_copy(maps_ref, maps_in, arrived.at[0]),
        pltpu.make_async_copy(probes_ref, probes_in, arrived.at[1]),
    ]
    for copy in copies:
        copy.start()
    for copy in copies:
        copy.wait()
    maps = maps_in[...]
    probes = probes_in[...]
    vox, cols = maps.shape[1], probes.shape[1]
    width = vox // pieces
    sums = jnp.sum(maps.astype(F32), axis=0, keepdims=True)
    probe_sums = jnp.sum(probes.astype(F32), axis=0, keepdims=True)
    product = lax.dot_general(maps, probes, (((0,), (0,)), ((), ())), preferred_element_type=F32)
    for k in range(pieces):
        base = k * (width + PAD)
        out_ref[base : base + width, :] = product[k * width : (k + 1) * width, :]
        out_ref[base + width : base + width + 1, :width] = sums[:, k * width : (k + 1) * width]
        out_ref[base + width + 1 : base + width + 2, :] = probe_sums


def sum_repeat_kernel(sources, copies, in_ref, out_ref):
    rows = in_ref.shape[0] // sources
    total = in_ref[0:rows, :]
    for k in range(1, sources):
        total = total + in_ref[k * rows : (k + 1) * rows, :]
    for k in range(copies):
        out_ref[k * rows : (k + 1) * rows, :] = total


def centre_kernel(sources, copies, subjects, in_ref, out_ref):
    rows = in_ref.shape[0] // sources
    width = rows - PAD
    total = in_ref[0:rows, :]
    for k in range(1, sources):
        total = total + in_ref[k * rows : (k + 1) * rows, :]
    mean = total[width : width + 1, :width] / subjects
    probe_sums = total[width + 1 : width + 2, :]
    square = (width, width)
    on_diagonal = lax.broadcasted_iota(jnp.int32, square, 0) == lax.broadcasted_iota(
        jnp.int32, square, 1
    )
    mean_column = jnp.sum(jnp.where(on_diagonal, mean, 0.0), axis=1, keepdims=True)
    piece = total[:width, :] - mean_column * probe_sums
    for k in range(copies):
        out_ref[k * rows : k * rows + width, :] = piece
        out_ref[k * rows + width : k * rows + width + 1, :width] = mean


def split_terms(value):
    terms = []
    for _ in range(3):
        term = value.astype(BF16)
        terms.append(term)
        value = value - term.astype(F32)
    return terms


def sketch_kernel(
    pieces, vox_total, pos_ref, maps_ref, w_ref, _, kept_ref, sent_ref, mean_ref, centered_ref, parts
):
    rows = w_ref.shape[0] // pieces
    width = rows - PAD

    @pl.when(pl.program_id(0) == 0)
    def _():
        for k in range(pieces):
            w = w_ref[k * rows : k * rows + width, :] * (1.0 / vox_total)
            for n, part in enumerate(split_terms(w)):
                parts[n, k * width : (k + 1) * width, :] = part
        mean_ref[...] = jnp.concatenate(
            [w_ref[k * rows + width : k * rows + width + 1, :width] for k in range(pieces)], axis=1
        )

    centered = (maps_ref[...].astype(F32) - mean_ref[...]).astype(BF16)
    centered_ref[...] = centered
    total = jnp.dot(centered, parts[0], preferred_element_type=F32)
    total += jnp.dot(centered, parts[1], preferred_element_type=F32)
    total += jnp.dot(centered, parts[2], preferred_element_type=F32)
    count, half = kept_ref.shape[0], kept_ref.shape[1]
    split = total.reshape(count, 2, half, total.shape[1])

    @pl.when(pos_ref[0] == 0)
    def _():
        kept_ref[...] = split[:, 0]
        sent_ref[...] = split[:, 1]

    @pl.when(pos_ref[0] == 1)
    def _():
        kept_ref[...] = split[:, 1]
        sent_ref[...] = split[:, 0]


def sort_kernel(shifts, pos_ref, *refs):
    count = len(shifts)
    pieces, (kept_ref, sent_ref, arrived) = refs[:count], refs[count:]
    groups = kept_ref.shape[0]
    total = 2 * groups
    for k, ((shift, start), piece) in enumerate(zip(shifts, pieces)):
        group = lax.rem(pos_ref[2] + (shift + total), total)
        mine = group // groups == pos_ref[0]
        place = lax.rem(group, groups)
        rows = piece.shape[0]

        @pl.when(mine)
        def _(k=k, piece=piece, place=place, start=start, rows=rows):
            target = kept_ref.at[place, pl.ds(start, rows)]
            pltpu.make_async_copy(piece, target, arrived.at[k]).start()

        @pl.when(jnp.logical_not(mine))
        def _(k=k, piece=piece, place=place, start=start, rows=rows):
            target = sent_ref.at[place, pl.ds(start, rows)]
            pltpu.make_async_copy(piece, target, arrived.at[k]).start()

    for k, ((_, start), piece) in enumerate(zip(shifts, pieces)):
        target = kept_ref.at[0, pl.ds(start, piece.shape[0])]
        pltpu.make_async_copy(piece, target, arrived.at[k]).wait()


def cross_kernel(subjects, copies, pos_ref, kept_ref, got_ref, _, out_ref, own_ref, __, full):
    sketch = kept_ref[...] + got_ref[...]
    groups, half, cols = sketch.shape
    flat = sketch.reshape(groups * half, cols)
    full[...] = lax.dot_general(
        flat, flat, (((0,), (0,)), ((), ())), precision=HIGHEST, preferred_element_type=F32
    ) * (1.0 / subjects)
    col = pos_ref[1]
    rows = out_ref.shape[0] // copies
    piece = full[pl.ds(pl.multiple_of(col * rows, rows), rows), :]
    for k in range(copies):
        out_ref[k * rows : (k + 1) * rows, :] = piece
    own_ref[...] = kept_ref[col] + got_ref[col]


def cholesky_kernel(block, cross_ref, own_ref, factor_ref, basis_ref, work):
    size = cross_ref.shape[0]
    mine = own_ref.shape[0]
    work[:, :size] = cross_ref[...]
    padded = jnp.concatenate([own_ref[...], jnp.zeros((128 - mine, size), F32)], axis=0)
    work[:, size:] = padded.T
    shape = (block, 128)
    row_id = lax.broadcasted_iota(jnp.int32, shape, 0)

    def spread(value):
        return jnp.broadcast_to(value, shape)

    for start in range(0, size, block):
        lane0 = start // 128 * 128
        chunks = [work[start : start + block, k : k + 128] for k in range(lane0, size + 128, 128)]
        first = start - lane0
        columns = [spread(chunks[0][:, first + j : first + j + 1]) for j in range(block)]
        scale = jnp.zeros(shape, F32)
        for i in range(block):
            pivot = spread(columns[i][i : i + 1, :])
            scale = jnp.where(row_id == i, lax.rsqrt(pivot), scale)
            if i < block - 1:
                weight = jnp.where(row_id > i, columns[i] * (1.0 / pivot), 0.0)
                for j in range(i + 1, block):
                    columns[j] = columns[j] - weight * spread(columns[j][i : i + 1, :])
                chunks = [c - weight * spread(c[i : i + 1, :]) for c in chunks]
        panel = jnp.concatenate([c * scale for c in chunks], axis=1)
        work[start : start + block, lane0:] = panel
        stop = start + block
        if stop < size:
            lane1 = stop // 128 * 128
            right = split_terms(panel[:, lane1 - lane0 :])
            left = [part[:, : size - lane1] for part in right]
            update = lax.dot_general(
                jnp.concatenate([left[k] for k in (0, 0, 1, 0, 2, 1)], axis=0),
                jnp.concatenate([right[k] for k in (0, 1, 0, 2, 0, 1)], axis=0),
                (((0,), (0,)), ((), ())),
                preferred_element_type=F32,
            )
            work[stop:, lane1:] = work[stop:, lane1:] - update[stop - lane1 :, :]
    square = (size, size)
    upper = lax.broadcasted_iota(jnp.int32, square, 0) <= lax.broadcasted_iota(jnp.int32, square, 1)
    factor_ref[...] = jnp.where(upper, work[:, :size], 0.0)
    basis_ref[...] = work[:, size:].T[:mine, :]


def gram_kernel(vox_total, own_ref, other_ref, col_own_ref, col_other_ref, means_ref, _, out_ref, done_ref, cols):
    half = own_ref.shape[1]

    @pl.when(pl.program_id(0) == 0)
    def _():
        for k, ref in enumerate((col_own_ref, col_other_ref)):
            mean = means_ref[k : k + 1, :]
            cols[:, k * half : (k + 1) * half] = (ref[...].astype(F32) - mean).astype(BF16)

    contract = (((1,), (1,)), ((), ()))
    tile = lax.dot_general(own_ref[...], cols[:, :half], contract, preferred_element_type=F32)
    tile += lax.dot_general(other_ref[...], cols[:, half:], contract, preferred_element_type=F32)
    tile = tile * (1.0 / vox_total)
    done_ref[...] = jnp.zeros(done_ref.shape, F32)
    rows = tile.shape[0]
    groups = tile.shape[1] // 128
    for a in range(groups):
        out_ref[pl.ds(a, rows, stride=groups), :] = tile[:, a * 128 : (a + 1) * 128]


def gram_part(vox_total, groups, part, before, own, other, col_own, col_other, means):
    rows, vox_half = own.shape
    tall = min(512, rows // 2)
    steps = rows // tall // 2
    row_spec = pl.BlockSpec((tall, vox_half), lambda i: (i + part * steps, 0))
    col_spec = pl.BlockSpec(col_own.shape, lambda i: (0, 0))
    return pl.pallas_call(
        functools.partial(gram_kernel, vox_total),
        grid=(steps,),
        in_specs=[
            row_spec,
            row_spec,
            col_spec,
            col_spec,
            pl.BlockSpec(means.shape, lambda i: (0, 0)),
            pl.BlockSpec(memory_space=pl.ANY),
        ],
        out_specs=[
            pl.BlockSpec((tall * groups, 128), lambda i: (i + part * steps, 0)),
            pl.BlockSpec((8, 128), lambda i: (0, 0)),
        ],
        out_shape=[sd((rows * groups, 128)), sd((8, 128))],
        scratch_shapes=[pltpu.VMEM((col_own.shape[0], vox_total), BF16)],
        input_output_aliases={} if before is None else {5: 0},
        compiler_params=LARGE,
    )(own, other, col_own, col_other, means, means if before is None else before)


def ring_step(up, down, axis, size, hops=1):
    ahead = [(i, (i + hops) % size) for i in range(size)]
    back = [(i, (i - hops) % size) for i in range(size)]
    return lax.ppermute(up, axis, ahead), lax.ppermute(down, axis, back)


def shards(maps, probes):
    sub_rows, vox_half = maps.shape
    width = probes.shape[1]
    row_count = lax.axis_size("row")
    col_count = lax.axis_size("col")
    vox_count = lax.axis_size("vox")
    subjects = sub_rows * row_count * col_count
    vox_total = vox_half * vox_count
    block_rows = sub_rows * col_count
    groups = row_count // vox_count
    col_pos = lax.axis_index("col")
    vox_pos = lax.axis_index("vox")
    pos = jnp.stack([vox_pos, col_pos, lax.axis_index("row")]).astype(jnp.int32)
    swap = [(0, 1), (1, 0)]

    def exchange(value, axis):
        return lax.all_to_all(value, axis, 0, 0, tiled=True)

    row_maps = lax.all_gather(maps, "col", axis=0, tiled=True)
    slice_rows = vox_half // col_count + PAD
    up, down = ring_step(maps, maps, "row", row_count)
    ring = [((0, 0), maps), ((-1, 0), up), ((1, 0), down)]
    up, down = ring_step(up, down, "row", row_count)
    (local,) = call(
        functools.partial(project_kernel, col_count),
        [sd((col_count * slice_rows, width))],
        maps,
        probes,
        in_specs=[pl.BlockSpec(memory_space=pl.ANY)] * 2,
        params=ALL,
        scratch_shapes=[
            pltpu.VMEM(maps.shape, BF16),
            pltpu.VMEM(probes.shape, BF16),
            pltpu.SemaphoreType.DMA((2,)),
        ],
    )
    (part,) = call(
        functools.partial(sum_repeat_kernel, col_count, row_count),
        [sd((row_count * slice_rows, width))],
        exchange(local, "col"),
        after=[up, down],
    )
    whole, up, down = call(
        functools.partial(centre_kernel, row_count, col_count, subjects),
        [sd((col_count * slice_rows, width))],
        exchange(part, "row"),
        carry=[up, down],
    )
    weights = exchange(whole, "col")
    ring += [((-2, 0), up), ((2, 0), down)]
    half_block = sub_rows // 2
    for k in range(3, row_count // 2):
        ahead, back = ring_step(up, down, "row", row_count, k - 2)
        ring += [((-k, 0), ahead), ((k, 0), back)]
    far = row_count // 2
    ahead, back = ring_step(up[:half_block], down[half_block:], "row", row_count, far - 2)
    ring += [((-far, 0), ahead), ((far, half_block), back)]
    group_shape = (groups, sub_rows, vox_half)
    anywhere = pl.BlockSpec(memory_space=pl.ANY)
    col_kept, col_sent = pl.pallas_call(
        functools.partial(sort_kernel, [key for key, _ in ring]),
        grid_spec=pltpu.PrefetchScalarGridSpec(
            num_scalar_prefetch=1,
            grid=(1,),
            in_specs=[anywhere] * len(ring),
            out_specs=[anywhere] * 2,
            scratch_shapes=[pltpu.SemaphoreType.DMA((len(ring),))],
        ),
        out_shape=[sd(group_shape, BF16)] * 2,
        cost_estimate=pl.CostEstimate(flops=0, bytes_accessed=1024, transcendentals=0),
        compiler_params=ALL,
    )(pos, *[piece for _, piece in ring])
    col_other = lax.ppermute(col_sent, "vox", swap)

    half_rows = sub_rows // vox_count
    step = min(4 * sub_rows, block_rows)
    half_spec = pl.BlockSpec((step // sub_rows, half_rows, width), lambda i, p: (i, 0, 0))
    kept, sent, mean, centered = pl.pallas_call(
        functools.partial(sketch_kernel, col_count, vox_total),
        grid_spec=pltpu.PrefetchScalarGridSpec(
            num_scalar_prefetch=1,
            grid=(block_rows // step,),
            in_specs=[
                pl.BlockSpec((step, vox_half), lambda i, p: (i, 0)),
                pl.BlockSpec((col_count * slice_rows, width), lambda i, p: (0, 0)),
                pl.BlockSpec(memory_space=pl.ANY),
            ],
            out_specs=[
                half_spec,
                half_spec,
                pl.BlockSpec((1, vox_half), lambda i, p: (0, 0)),
                pl.BlockSpec((step, vox_half), lambda i, p: (i, 0)),
            ],
            scratch_shapes=[pltpu.VMEM((3, vox_half, width), BF16)],
        ),
        out_shape=[
            sd((col_count, half_rows, width)),
            sd((col_count, half_rows, width)),
            sd((1, vox_half)),
            sd((block_rows, vox_half), BF16),
        ],
        compiler_params=LARGE,
    )(pos, row_maps, weights, col_other)
    got = lax.ppermute(sent, "vox", swap)
    cross_rows = width // col_count
    copies = row_count * vox_count
    slices, own, centered = pl.pallas_call(
        functools.partial(cross_kernel, subjects, copies),
        grid_spec=pltpu.PrefetchScalarGridSpec(
            num_scalar_prefetch=1,
            grid=(1,),
            in_specs=[
                pl.BlockSpec((col_count, half_rows, width), lambda i, p: (0, 0, 0)),
                pl.BlockSpec((col_count, half_rows, width), lambda i, p: (0, 0, 0)),
                pl.BlockSpec(memory_space=pl.ANY),
            ],
            out_specs=[
                pl.BlockSpec((copies * cross_rows, width), lambda i, p: (0, 0)),
                pl.BlockSpec((half_rows, width), lambda i, p: (0, 0)),
                pl.BlockSpec(memory_space=pl.ANY),
            ],
            scratch_shapes=[pltpu.VMEM((width, width), F32)],
        ),
        out_shape=[
            sd((copies * cross_rows, width)),
            sd((half_rows, width)),
            sd((block_rows, vox_half), BF16),
        ],
        input_output_aliases={3: 2},
        compiler_params=PARAMS,
    )(pos, kept, got, centered)
    other = lax.ppermute(centered, "vox", swap)
    means = jnp.concatenate([mean, lax.ppermute(mean, "vox", swap)], axis=0)
    own_cols = groups * sub_rows
    flat = (own_cols, vox_half)
    operands = (centered, other, col_kept.reshape(flat), col_other.reshape(flat), means)
    gram, first = gram_part(vox_total, groups, 0, None, *operands)
    (summed,) = call(
        functools.partial(sum_repeat_kernel, copies, col_count),
        [sd((width, width))],
        exchange(slices, ("row", "vox")),
        after=[first],
    )
    cross = exchange(summed, "col")
    gram, second = gram_part(vox_total, groups, 1, gram, *operands)
    factor, basis = call(
        functools.partial(cholesky_kernel, 16),
        [sd((width, width)), sd((half_rows, width))],
        cross,
        own,
        after=[second],
        scratch_shapes=[pltpu.VMEM((width, width + 128), F32)],
    )
    return gram.reshape(block_rows, groups, 1, sub_rows), basis, factor


def solution(mesh):
    placed = (P(("row", "col"), "vox"), P(("row", "col"), None))
    return jax.shard_map(
        shards,
        mesh=mesh,
        in_specs=placed,
        out_specs=(P("row", "vox", "col", None), P(("row", "col", "vox"), None), P()),
        check_vma=False,
    )
```

```python
import functools

import jax
import jax.numpy as jnp
from jax import lax
from jax.experimental import pallas as pl
from jax.experimental.pallas import tpu as pltpu
from jax.sharding import PartitionSpec as P

F32 = jnp.float32
BF16 = jnp.bfloat16
HIGHEST = lax.Precision.HIGHEST
PAD = 8
PARAMS = pltpu.CompilerParams(vmem_limit_bytes=24 * 1024 * 1024)
LARGE = pltpu.CompilerParams(vmem_limit_bytes=48 * 1024 * 1024)
ALL = pltpu.CompilerParams(vmem_limit_bytes=58 * 1024 * 1024)


def call(kernel, out_shape, *args, after=(), carry=(), params=PARAMS, **kw):
    count, outs = len(args), len(out_shape)
    others = len(after) + len(carry)

    def body(*refs):
        kernel(*refs[:count], *refs[count + others :][:outs], *refs[count + others + outs + len(carry) :])

    anywhere = pl.BlockSpec(memory_space=pl.ANY)
    vmem = pl.BlockSpec(memory_space=pltpu.VMEM)
    return pl.pallas_call(
        body,
        out_shape=[*out_shape, *[sd(x.shape, x.dtype) for x in carry]],
        in_specs=kw.pop("in_specs", [vmem] * count) + [anywhere] * others,
        out_specs=[vmem] * outs + [anywhere] * len(carry),
        input_output_aliases={count + len(after) + k: outs + k for k in range(len(carry))},
        compiler_params=params,
        **kw,
    )(*args, *after, *carry)


def sd(shape, dtype=F32):
    return jax.ShapeDtypeStruct(shape, dtype)


def project_kernel(pieces, maps_ref, probes_ref, out_ref, maps_in, probes_in, arrived):
    copies = [
        pltpu.make_async_copy(maps_ref, maps_in, arrived.at[0]),
        pltpu.make_async_copy(probes_ref, probes_in, arrived.at[1]),
    ]
    for copy in copies:
        copy.start()
    for copy in copies:
        copy.wait()
    maps = maps_in[...]
    probes = probes_in[...]
    vox, cols = maps.shape[1], probes.shape[1]
    width = vox // pieces
    sums = jnp.sum(maps.astype(F32), axis=0, keepdims=True)
    probe_sums = jnp.sum(probes.astype(F32), axis=0, keepdims=True)
    product = lax.dot_general(maps, probes, (((0,), (0,)), ((), ())), preferred_element_type=F32)
    for k in range(pieces):
        base = k * (width + PAD)
        out_ref[base : base + width, :] = product[k * width : (k + 1) * width, :]
        out_ref[base + width : base + width + 1, :width] = sums[:, k * width : (k + 1) * width]
        out_ref[base + width + 1 : base + width + 2, :] = probe_sums


def sum_repeat_kernel(sources, copies, in_ref, out_ref):
    rows = in_ref.shape[0] // sources
    total = in_ref[0:rows, :]
    for k in range(1, sources):
        total = total + in_ref[k * rows : (k + 1) * rows, :]
    for k in range(copies):
        out_ref[k * rows : (k + 1) * rows, :] = total


def centre_kernel(
    sources,
    copies,
    subjects,
    in_ref,
    up1_ref,
    down1_ref,
    up2_ref,
    down2_ref,
    out_ref,
    up_ref,
    down_ref,
):
    sub_rows = up1_ref.shape[0]
    half_block = sub_rows // 2
    up_ref[:sub_rows, :] = up1_ref[...]
    up_ref[sub_rows:, :] = up2_ref[:half_block, :]
    down_ref[:sub_rows, :] = down1_ref[...]
    down_ref[sub_rows:, :] = down2_ref[half_block:, :]
    rows = in_ref.shape[0] // sources
    width = rows - PAD
    total = in_ref[0:rows, :]
    for k in range(1, sources):
        total = total + in_ref[k * rows : (k + 1) * rows, :]
    mean = total[width : width + 1, :width] / subjects
    probe_sums = total[width + 1 : width + 2, :]
    square = (width, width)
    on_diagonal = lax.broadcasted_iota(jnp.int32, square, 0) == lax.broadcasted_iota(
        jnp.int32, square, 1
    )
    mean_column = jnp.sum(jnp.where(on_diagonal, mean, 0.0), axis=1, keepdims=True)
    piece = total[:width, :] - mean_column * probe_sums
    for k in range(copies):
        out_ref[k * rows : k * rows + width, :] = piece
        out_ref[k * rows + width : k * rows + width + 1, :width] = mean


def split_terms(value, count=3):
    terms = []
    for _ in range(count):
        term = value.astype(BF16)
        terms.append(term)
        value = value - term.astype(F32)
    return terms


def sketch_kernel(
    pieces, vox_total, pos_ref, maps_ref, w_ref, _, kept_ref, sent_ref, mean_ref, centered_ref, parts
):
    rows = w_ref.shape[0] // pieces
    width = rows - PAD

    @pl.when(pl.program_id(0) == 0)
    def _():
        for k in range(pieces):
            w = w_ref[k * rows : k * rows + width, :] * (1.0 / vox_total)
            for n, part in enumerate(split_terms(w, 2)):
                parts[n, k * width : (k + 1) * width, :] = part
        mean_ref[...] = jnp.concatenate(
            [w_ref[k * rows + width : k * rows + width + 1, :width] for k in range(pieces)], axis=1
        )

    centered = (maps_ref[...].astype(F32) - mean_ref[...]).astype(BF16)
    centered_ref[...] = centered
    total = jnp.dot(centered, parts[0], preferred_element_type=F32)
    total += jnp.dot(centered, parts[1], preferred_element_type=F32)
    count, half = kept_ref.shape[0], kept_ref.shape[1]
    split = total.reshape(count, 2, half, total.shape[1])

    @pl.when(pos_ref[0] == 0)
    def _():
        kept_ref[...] = split[:, 0]
        sent_ref[...] = split[:, 1]

    @pl.when(pos_ref[0] == 1)
    def _():
        kept_ref[...] = split[:, 1]
        sent_ref[...] = split[:, 0]


def sort_kernel(places, pos_ref, *refs):
    pieces, kept_ref, sent_ref = refs[:-2], refs[-2], refs[-1]
    groups = kept_ref.shape[0]
    total = 2 * groups
    for index, source, rows, shift, target in places:
        group = lax.rem(pos_ref[2] + (shift + total), total)
        mine = group // groups == pos_ref[0]
        place = lax.rem(group, groups)
        piece = pieces[index]

        @pl.when(mine)
        def _(piece=piece, source=source, rows=rows, place=place, target=target):
            kept_ref[place, target : target + rows, :] = piece[source : source + rows, :]

        @pl.when(jnp.logical_not(mine))
        def _(piece=piece, source=source, rows=rows, place=place, target=target):
            sent_ref[place, target : target + rows, :] = piece[source : source + rows, :]


def cross_kernel(subjects, copies, pos_ref, kept_ref, got_ref, _, out_ref, own_ref, __, full):
    sketch = kept_ref[...] + got_ref[...]
    groups, half, cols = sketch.shape
    flat = sketch.reshape(groups * half, cols)
    full[...] = lax.dot_general(
        flat, flat, (((0,), (0,)), ((), ())), precision=HIGHEST, preferred_element_type=F32
    ) * (1.0 / subjects)
    col = pos_ref[1]
    rows = out_ref.shape[0] // copies
    piece = full[pl.ds(pl.multiple_of(col * rows, rows), rows), :]
    for k in range(copies):
        out_ref[k * rows : (k + 1) * rows, :] = piece
    own_ref[...] = kept_ref[col] + got_ref[col]


def cholesky_kernel(block, cross_ref, own_ref, factor_ref, basis_ref, work):
    size = cross_ref.shape[0]
    mine = own_ref.shape[0]
    work[:, :size] = cross_ref[...]
    padded = jnp.concatenate([own_ref[...], jnp.zeros((128 - mine, size), F32)], axis=0)
    work[:, size:] = padded.T
    shape = (block, 128)
    row_id = lax.broadcasted_iota(jnp.int32, shape, 0)

    def spread(value):
        return jnp.broadcast_to(value, shape)

    for start in range(0, size, block):
        lane0 = start // 128 * 128
        chunks = [work[start : start + block, k : k + 128] for k in range(lane0, size + 128, 128)]
        first = start - lane0
        columns = [spread(chunks[0][:, first + j : first + j + 1]) for j in range(block)]
        scale = jnp.zeros(shape, F32)
        for i in range(block):
            pivot = spread(columns[i][i : i + 1, :])
            scale = jnp.where(row_id == i, lax.rsqrt(pivot), scale)
            if i < block - 1:
                weight = jnp.where(row_id > i, columns[i] * (1.0 / pivot), 0.0)
                for j in range(i + 1, block):
                    columns[j] = columns[j] - weight * spread(columns[j][i : i + 1, :])
                chunks = [c - weight * spread(c[i : i + 1, :]) for c in chunks]
        panel = jnp.concatenate([c * scale for c in chunks], axis=1)
        work[start : start + block, lane0:] = panel
        stop = start + block
        if stop < size:
            lane1 = stop // 128 * 128
            right = split_terms(panel[:, lane1 - lane0 :])
            left = [part[:, : size - lane1] for part in right]
            update = lax.dot_general(
                jnp.concatenate([left[k] for k in (0, 0, 1, 0, 2, 1)], axis=0),
                jnp.concatenate([right[k] for k in (0, 1, 0, 2, 0, 1)], axis=0),
                (((0,), (0,)), ((), ())),
                preferred_element_type=F32,
            )
            work[stop:, lane1:] = work[stop:, lane1:] - update[stop - lane1 :, :]
    square = (size, size)
    upper = lax.broadcasted_iota(jnp.int32, square, 0) <= lax.broadcasted_iota(jnp.int32, square, 1)
    factor_ref[...] = jnp.where(upper, work[:, :size], 0.0)
    basis_ref[...] = work[:, size:].T[:mine, :]


def gram_kernel(vox_total, own_ref, other_ref, col_own_ref, col_other_ref, means_ref, _, out_ref, done_ref, cols):
    half = own_ref.shape[1]

    @pl.when(pl.program_id(0) == 0)
    def _():
        for k, ref in enumerate((col_own_ref, col_other_ref)):
            mean = means_ref[k : k + 1, :]
            cols[:, k * half : (k + 1) * half] = (ref[...].astype(F32) - mean).astype(BF16)

    contract = (((1,), (1,)), ((), ()))
    tile = lax.dot_general(own_ref[...], cols[:, :half], contract, preferred_element_type=F32)
    tile += lax.dot_general(other_ref[...], cols[:, half:], contract, preferred_element_type=F32)
    tile = tile * (1.0 / vox_total)
    done_ref[...] = jnp.zeros(done_ref.shape, F32)
    rows = tile.shape[0]
    groups = tile.shape[1] // 128
    for a in range(groups):
        out_ref[pl.ds(a, rows, stride=groups), :] = tile[:, a * 128 : (a + 1) * 128]


def gram_part(vox_total, groups, part, before, own, other, col_own, col_other, means):
    rows, vox_half = own.shape
    tall = min(512, rows // 2)
    steps = rows // tall // 2
    row_spec = pl.BlockSpec((tall, vox_half), lambda i: (i + part * steps, 0))
    col_spec = pl.BlockSpec(col_own.shape, lambda i: (0, 0))
    return pl.pallas_call(
        functools.partial(gram_kernel, vox_total),
        grid=(steps,),
        in_specs=[
            row_spec,
            row_spec,
            col_spec,
            col_spec,
            pl.BlockSpec(means.shape, lambda i: (0, 0)),
            pl.BlockSpec(memory_space=pl.ANY),
        ],
        out_specs=[
            pl.BlockSpec((tall * groups, 128), lambda i: (i + part * steps, 0)),
            pl.BlockSpec((8, 128), lambda i: (0, 0)),
        ],
        out_shape=[sd((rows * groups, 128)), sd((8, 128))],
        scratch_shapes=[pltpu.VMEM((col_own.shape[0], vox_total), BF16)],
        input_output_aliases={} if before is None else {5: 0},
        compiler_params=LARGE,
    )(own, other, col_own, col_other, means, means if before is None else before)


def ring_step(up, down, axis, size, hops=1):
    ahead = [(i, (i + hops) % size) for i in range(size)]
    back = [(i, (i - hops) % size) for i in range(size)]
    return lax.ppermute(up, axis, ahead), lax.ppermute(down, axis, back)


def shards(maps, probes):
    sub_rows, vox_half = maps.shape
    width = probes.shape[1]
    row_count = lax.axis_size("row")
    col_count = lax.axis_size("col")
    vox_count = lax.axis_size("vox")
    subjects = sub_rows * row_count * col_count
    vox_total = vox_half * vox_count
    block_rows = sub_rows * col_count
    groups = row_count // vox_count
    col_pos = lax.axis_index("col")
    vox_pos = lax.axis_index("vox")
    pos = jnp.stack([vox_pos, col_pos, lax.axis_index("row")]).astype(jnp.int32)
    swap = [(0, 1), (1, 0)]

    def exchange(value, axis):
        return lax.all_to_all(value, axis, 0, 0, tiled=True)

    row_maps = lax.all_gather(maps, "col", axis=0, tiled=True)
    slice_rows = vox_half // col_count + PAD
    up1, down1 = ring_step(maps, maps, "row", row_count)
    up2, down2 = ring_step(up1, down1, "row", row_count)
    (local,) = call(
        functools.partial(project_kernel, col_count),
        [sd((col_count * slice_rows, width))],
        maps,
        probes,
        in_specs=[pl.BlockSpec(memory_space=pl.ANY)] * 2,
        params=ALL,
        scratch_shapes=[
            pltpu.VMEM(maps.shape, BF16),
            pltpu.VMEM(probes.shape, BF16),
            pltpu.SemaphoreType.DMA((2,)),
        ],
    )
    (part,) = call(
        functools.partial(sum_repeat_kernel, col_count, row_count),
        [sd((row_count * slice_rows, width))],
        exchange(local, "col"),
        after=[up1, down1, up2, down2],
    )
    half_block = sub_rows // 2
    far_block = (sub_rows + half_block, vox_half)
    whole, up, down = call(
        functools.partial(centre_kernel, row_count, col_count, subjects),
        [sd((col_count * slice_rows, width)), sd(far_block, BF16), sd(far_block, BF16)],
        exchange(part, "row"),
        up1,
        down1,
        up2,
        down2,
    )
    weights = exchange(whole, "col")
    up3, down3 = ring_step(up, down, "row", row_count, 2)
    ring = [maps, up1, down1, up2, down2, up3, down3]
    places = [(k, 0, sub_rows, shift, 0) for k, shift in enumerate((0, -1, 1, -2, 2, -3, 3))]
    places += [(5, sub_rows, half_block, -4, 0), (6, sub_rows, half_block, 4, half_block)]
    group_shape = (groups, sub_rows, vox_half)
    whole_block = pl.BlockSpec(group_shape, lambda i, p: (0, 0, 0))
    col_kept, col_sent = pl.pallas_call(
        functools.partial(sort_kernel, places),
        grid_spec=pltpu.PrefetchScalarGridSpec(
            num_scalar_prefetch=1,
            grid=(1,),
            in_specs=[pl.BlockSpec(piece.shape, lambda i, p: (0, 0)) for piece in ring],
            out_specs=[whole_block, whole_block],
        ),
        out_shape=[sd(group_shape, BF16)] * 2,
        compiler_params=ALL,
    )(pos, *ring)
    col_other = lax.ppermute(col_sent, "vox", swap)

    half_rows = sub_rows // vox_count
    step = min(4 * sub_rows, block_rows)
    half_spec = pl.BlockSpec((step // sub_rows, half_rows, width), lambda i, p: (i, 0, 0))
    kept, sent, mean, centered = pl.pallas_call(
        functools.partial(sketch_kernel, col_count, vox_total),
        grid_spec=pltpu.PrefetchScalarGridSpec(
            num_scalar_prefetch=1,
            grid=(block_rows // step,),
            in_specs=[
                pl.BlockSpec((step, vox_half), lambda i, p: (i, 0)),
                pl.BlockSpec((col_count * slice_rows, width), lambda i, p: (0, 0)),
                pl.BlockSpec(memory_space=pl.ANY),
            ],
            out_specs=[
                half_spec,
                half_spec,
                pl.BlockSpec((1, vox_half), lambda i, p: (0, 0)),
                pl.BlockSpec((step, vox_half), lambda i, p: (i, 0)),
            ],
            scratch_shapes=[pltpu.VMEM((2, vox_half, width), BF16)],
        ),
        out_shape=[
            sd((col_count, half_rows, width)),
            sd((col_count, half_rows, width)),
            sd((1, vox_half)),
            sd((block_rows, vox_half), BF16),
        ],
        compiler_params=LARGE,
    )(pos, row_maps, weights, col_other)
    got = lax.ppermute(sent, "vox", swap)
    cross_rows = width // col_count
    copies = row_count * vox_count
    slices, own, centered = pl.pallas_call(
        functools.partial(cross_kernel, subjects, copies),
        grid_spec=pltpu.PrefetchScalarGridSpec(
            num_scalar_prefetch=1,
            grid=(1,),
            in_specs=[
                pl.BlockSpec((col_count, half_rows, width), lambda i, p: (0, 0, 0)),
                pl.BlockSpec((col_count, half_rows, width), lambda i, p: (0, 0, 0)),
                pl.BlockSpec(memory_space=pl.ANY),
            ],
            out_specs=[
                pl.BlockSpec((copies * cross_rows, width), lambda i, p: (0, 0)),
                pl.BlockSpec((half_rows, width), lambda i, p: (0, 0)),
                pl.BlockSpec(memory_space=pl.ANY),
            ],
            scratch_shapes=[pltpu.VMEM((width, width), F32)],
        ),
        out_shape=[
            sd((copies * cross_rows, width)),
            sd((half_rows, width)),
            sd((block_rows, vox_half), BF16),
        ],
        input_output_aliases={3: 2},
        compiler_params=PARAMS,
    )(pos, kept, got, centered)
    other = lax.ppermute(centered, "vox", swap)
    means = jnp.concatenate([mean, lax.ppermute(mean, "vox", swap)], axis=0)
    own_cols = groups * sub_rows
    flat = (own_cols, vox_half)
    operands = (centered, other, col_kept.reshape(flat), col_other.reshape(flat), means)
    gram, first = gram_part(vox_total, groups, 0, None, *operands)
    (summed,) = call(
        functools.partial(sum_repeat_kernel, copies, col_count),
        [sd((width, width))],
        exchange(slices, ("row", "vox")),
        after=[first],
    )
    cross = exchange(summed, "col")
    gram, second = gram_part(vox_total, groups, 1, gram, *operands)
    factor, basis = call(
        functools.partial(cholesky_kernel, 16),
        [sd((width, width)), sd((half_rows, width))],
        cross,
        own,
        after=[second],
        scratch_shapes=[pltpu.VMEM((width, width + 128), F32)],
    )
    return gram.reshape(block_rows, groups, 1, sub_rows), basis, factor


def solution(mesh):
    placed = (P(("row", "col"), "vox"), P(("row", "col"), None))
    return jax.shard_map(
        shards,
        mesh=mesh,
        in_specs=placed,
        out_specs=(P("row", "vox", "col", None), P(("row", "col", "vox"), None), P()),
        check_vma=False,
    )
```

```python
import functools

import jax
import jax.numpy as jnp
from jax import lax
from jax.experimental import pallas as pl
from jax.experimental.pallas import tpu as pltpu
from jax.sharding import PartitionSpec as P

F32 = jnp.float32
BF16 = jnp.bfloat16
HIGHEST = lax.Precision.HIGHEST
PAD = 8
PARAMS = pltpu.CompilerParams(vmem_limit_bytes=24 * 1024 * 1024)
LARGE = pltpu.CompilerParams(vmem_limit_bytes=48 * 1024 * 1024)
ALL = pltpu.CompilerParams(vmem_limit_bytes=58 * 1024 * 1024)


def call(kernel, out_shape, *args, after=(), carry=(), params=PARAMS, **kw):
    count, outs = len(args), len(out_shape)
    others = len(after) + len(carry)

    def body(*refs):
        kernel(*refs[:count], *refs[count + others :][:outs], *refs[count + others + outs + len(carry) :])

    anywhere = pl.BlockSpec(memory_space=pl.ANY)
    vmem = pl.BlockSpec(memory_space=pltpu.VMEM)
    return pl.pallas_call(
        body,
        out_shape=[*out_shape, *[sd(x.shape, x.dtype) for x in carry]],
        in_specs=kw.pop("in_specs", [vmem] * count) + [anywhere] * others,
        out_specs=[vmem] * outs + [anywhere] * len(carry),
        input_output_aliases={count + len(after) + k: outs + k for k in range(len(carry))},
        compiler_params=params,
        **kw,
    )(*args, *after, *carry)


def sd(shape, dtype=F32):
    return jax.ShapeDtypeStruct(shape, dtype)


def project_kernel(pieces, maps_ref, probes_ref, out_ref, maps_in, probes_in, arrived):
    copies = [
        pltpu.make_async_copy(maps_ref, maps_in, arrived.at[0]),
        pltpu.make_async_copy(probes_ref, probes_in, arrived.at[1]),
    ]
    for copy in copies:
        copy.start()
    for copy in copies:
        copy.wait()
    maps = maps_in[...]
    probes = probes_in[...]
    vox, cols = maps.shape[1], probes.shape[1]
    width = vox // pieces
    sums = jnp.sum(maps.astype(F32), axis=0, keepdims=True)
    probe_sums = jnp.sum(probes.astype(F32), axis=0, keepdims=True)
    product = lax.dot_general(maps, probes, (((0,), (0,)), ((), ())), preferred_element_type=F32)
    for k in range(pieces):
        base = k * (width + PAD)
        out_ref[base : base + width, :] = product[k * width : (k + 1) * width, :]
        out_ref[base + width : base + width + 1, :width] = sums[:, k * width : (k + 1) * width]
        out_ref[base + width + 1 : base + width + 2, :] = probe_sums


def sum_repeat_kernel(sources, copies, in_ref, out_ref):
    rows = in_ref.shape[0] // sources
    total = in_ref[0:rows, :]
    for k in range(1, sources):
        total = total + in_ref[k * rows : (k + 1) * rows, :]
    for k in range(copies):
        out_ref[k * rows : (k + 1) * rows, :] = total


def centre_kernel(
    sources,
    copies,
    subjects,
    in_ref,
    up1_ref,
    down1_ref,
    up2_ref,
    down2_ref,
    out_ref,
    up_ref,
    down_ref,
):
    sub_rows = up1_ref.shape[0]
    half_block = sub_rows // 2
    up_ref[:sub_rows, :] = up1_ref[...]
    up_ref[sub_rows:, :] = up2_ref[:half_block, :]
    down_ref[:sub_rows, :] = down1_ref[...]
    down_ref[sub_rows:, :] = down2_ref[half_block:, :]
    rows = in_ref.shape[0] // sources
    width = rows - PAD
    total = in_ref[0:rows, :]
    for k in range(1, sources):
        total = total + in_ref[k * rows : (k + 1) * rows, :]
    mean = total[width : width + 1, :width] / subjects
    probe_sums = total[width + 1 : width + 2, :]
    square = (width, width)
    on_diagonal = lax.broadcasted_iota(jnp.int32, square, 0) == lax.broadcasted_iota(
        jnp.int32, square, 1
    )
    mean_column = jnp.sum(jnp.where(on_diagonal, mean, 0.0), axis=1, keepdims=True)
    piece = total[:width, :] - mean_column * probe_sums
    for k in range(copies):
        out_ref[k * rows : k * rows + width, :] = piece
        out_ref[k * rows + width : k * rows + width + 1, :width] = mean


def split_terms(value, count=3):
    terms = []
    for _ in range(count):
        term = value.astype(BF16)
        terms.append(term)
        value = value - term.astype(F32)
    return terms


def sketch_kernel(
    pieces, vox_total, maps_ref, w_ref, _, kept_ref, sent_ref, mean_ref, centered_ref, parts
):
    rows = w_ref.shape[0] // pieces
    width = rows - PAD

    @pl.when(pl.program_id(0) == 0)
    def _():
        for k in range(pieces):
            w = w_ref[k * rows : k * rows + width, :] * (1.0 / vox_total)
            for n, part in enumerate(split_terms(w, 2)):
                parts[n, k * width : (k + 1) * width, :] = part
        mean_ref[...] = jnp.concatenate(
            [w_ref[k * rows + width : k * rows + width + 1, :width] for k in range(pieces)], axis=1
        )

    centered = (maps_ref[...].astype(F32) - mean_ref[...]).astype(BF16)
    centered_ref[...] = centered
    total = jnp.dot(centered, parts[0], preferred_element_type=F32)
    total += jnp.dot(centered, parts[1], preferred_element_type=F32)
    count, half = kept_ref.shape[0], kept_ref.shape[1]
    split = total.reshape(count, 2, half, total.shape[1])

    @pl.when(lax.axis_index("vox") == 0)
    def _():
        kept_ref[...] = split[:, 0]
        sent_ref[...] = split[:, 1]

    @pl.when(lax.axis_index("vox") == 1)
    def _():
        kept_ref[...] = split[:, 1]
        sent_ref[...] = split[:, 0]


def sort_kernel(places, *refs):
    pieces, (kept_ref, sent_ref, done_ref) = refs[:-3], refs[-3:]
    done_ref[...] = jnp.zeros(done_ref.shape, F32)
    groups = kept_ref.shape[0]
    total = 2 * groups
    for index, source, rows, shift, target in places:
        group = lax.rem(lax.axis_index("row") + (shift + total), total)
        mine = group // groups == lax.axis_index("vox")
        place = lax.rem(group, groups)
        piece = pieces[index]

        @pl.when(mine)
        def _(piece=piece, source=source, rows=rows, place=place, target=target):
            kept_ref[place, target : target + rows, :] = piece[source : source + rows, :]

        @pl.when(jnp.logical_not(mine))
        def _(piece=piece, source=source, rows=rows, place=place, target=target):
            sent_ref[place, target : target + rows, :] = piece[source : source + rows, :]


def cross_kernel(subjects, copies, kept_ref, got_ref, _, __, out_ref, own_ref, ___, ____, full):
    sketch = kept_ref[...] + got_ref[...]
    groups, half, cols = sketch.shape
    flat = sketch.reshape(groups * half, cols)
    full[...] = lax.dot_general(
        flat, flat, (((0,), (0,)), ((), ())), precision=HIGHEST, preferred_element_type=F32
    ) * (1.0 / subjects)
    col = lax.axis_index("col")
    rows = out_ref.shape[0] // copies
    piece = full[pl.ds(pl.multiple_of(col * rows, rows), rows), :]
    for k in range(copies):
        out_ref[k * rows : (k + 1) * rows, :] = piece
    own_ref[...] = kept_ref[col] + got_ref[col]


def cholesky_kernel(block, cross_ref, own_ref, factor_ref, basis_ref, work):
    size = cross_ref.shape[0]
    mine = own_ref.shape[0]
    work[:, :size] = cross_ref[...]
    padded = jnp.concatenate([own_ref[...], jnp.zeros((128 - mine, size), F32)], axis=0)
    work[:, size:] = padded.T
    shape = (block, 128)
    row_id = lax.broadcasted_iota(jnp.int32, shape, 0)

    def spread(value):
        return jnp.broadcast_to(value, shape)

    for start in range(0, size, block):
        lane0 = start // 128 * 128
        chunks = [work[start : start + block, k : k + 128] for k in range(lane0, size + 128, 128)]
        first = start - lane0
        columns = [spread(chunks[0][:, first + j : first + j + 1]) for j in range(block)]
        scale = jnp.zeros(shape, F32)
        for i in range(block):
            pivot = spread(columns[i][i : i + 1, :])
            scale = jnp.where(row_id == i, lax.rsqrt(pivot), scale)
            if i < block - 1:
                weight = jnp.where(row_id > i, columns[i] * (1.0 / pivot), 0.0)
                for j in range(i + 1, block):
                    columns[j] = columns[j] - weight * spread(columns[j][i : i + 1, :])
                chunks = [c - weight * spread(c[i : i + 1, :]) for c in chunks]
        panel = jnp.concatenate([c * scale for c in chunks], axis=1)
        work[start : start + block, lane0:] = panel
        stop = start + block
        if stop < size:
            lane1 = stop // 128 * 128
            right = split_terms(panel[:, lane1 - lane0 :])
            left = [part[:, : size - lane1] for part in right]
            update = lax.dot_general(
                jnp.concatenate([left[k] for k in (0, 0, 1, 0, 2, 1)], axis=0),
                jnp.concatenate([right[k] for k in (0, 1, 0, 2, 0, 1)], axis=0),
                (((0,), (0,)), ((), ())),
                preferred_element_type=F32,
            )
            work[stop:, lane1:] = work[stop:, lane1:] - update[stop - lane1 :, :]
    square = (size, size)
    upper = lax.broadcasted_iota(jnp.int32, square, 0) <= lax.broadcasted_iota(jnp.int32, square, 1)
    factor_ref[...] = jnp.where(upper, work[:, :size], 0.0)
    basis_ref[...] = work[:, size:].T[:mine, :]


def gram_kernel(vox_total, own_ref, other_ref, col_own_ref, col_other_ref, means_ref, _, out_ref, done_ref, cols):
    half = own_ref.shape[1]

    @pl.when(pl.program_id(0) == 0)
    def _():
        for k, ref in enumerate((col_own_ref, col_other_ref)):
            mean = means_ref[k : k + 1, :]
            cols[:, k * half : (k + 1) * half] = (ref[...].astype(F32) - mean).astype(BF16)

    contract = (((1,), (1,)), ((), ()))
    tile = lax.dot_general(own_ref[...], cols[:, :half], contract, preferred_element_type=F32)
    tile += lax.dot_general(other_ref[...], cols[:, half:], contract, preferred_element_type=F32)
    tile = tile * (1.0 / vox_total)
    done_ref[...] = jnp.zeros(done_ref.shape, F32)
    rows = tile.shape[0]
    groups = tile.shape[1] // 128
    for a in range(groups):
        out_ref[pl.ds(a, rows, stride=groups), :] = tile[:, a * 128 : (a + 1) * 128]


def gram_part(vox_total, groups, part, before, own, other, col_own, col_other, means):
    rows, vox_half = own.shape
    tall = min(512, rows // 2)
    steps = rows // tall // 2
    row_spec = pl.BlockSpec((tall, vox_half), lambda i: (i + part * steps, 0))
    col_spec = pl.BlockSpec(col_own.shape, lambda i: (0, 0))
    return pl.pallas_call(
        functools.partial(gram_kernel, vox_total),
        grid=(steps,),
        in_specs=[
            row_spec,
            row_spec,
            col_spec,
            col_spec,
            pl.BlockSpec(means.shape, lambda i: (0, 0)),
            pl.BlockSpec(memory_space=pl.ANY),
        ],
        out_specs=[
            pl.BlockSpec((tall * groups, 128), lambda i: (i + part * steps, 0)),
            pl.BlockSpec((8, 128), lambda i: (0, 0)),
        ],
        out_shape=[sd((rows * groups, 128)), sd((8, 128))],
        scratch_shapes=[pltpu.VMEM((col_own.shape[0], vox_total), BF16)],
        input_output_aliases={} if before is None else {5: 0},
        compiler_params=LARGE,
    )(own, other, col_own, col_other, means, means if before is None else before)


def ring_step(up, down, axis, size, hops=1):
    ahead = [(i, (i + hops) % size) for i in range(size)]
    back = [(i, (i - hops) % size) for i in range(size)]
    return lax.ppermute(up, axis, ahead), lax.ppermute(down, axis, back)


def shards(maps, probes):
    sub_rows, vox_half = maps.shape
    width = probes.shape[1]
    row_count = lax.axis_size("row")
    col_count = lax.axis_size("col")
    vox_count = lax.axis_size("vox")
    subjects = sub_rows * row_count * col_count
    vox_total = vox_half * vox_count
    block_rows = sub_rows * col_count
    groups = row_count // vox_count
    swap = [(0, 1), (1, 0)]

    def exchange(value, axis):
        return lax.all_to_all(value, axis, 0, 0, tiled=True)

    row_maps = lax.all_gather(maps, "col", axis=0, tiled=True)
    slice_rows = vox_half // col_count + PAD
    up1, down1 = ring_step(maps, maps, "row", row_count)
    up2, down2 = ring_step(up1, down1, "row", row_count)
    (local,) = call(
        functools.partial(project_kernel, col_count),
        [sd((col_count * slice_rows, width))],
        maps,
        probes,
        in_specs=[pl.BlockSpec(memory_space=pl.ANY)] * 2,
        params=ALL,
        scratch_shapes=[
            pltpu.VMEM(maps.shape, BF16),
            pltpu.VMEM(probes.shape, BF16),
            pltpu.SemaphoreType.DMA((2,)),
        ],
    )
    (part,) = call(
        functools.partial(sum_repeat_kernel, col_count, row_count),
        [sd((row_count * slice_rows, width))],
        exchange(local, "col"),
        after=[up1, down1, up2, down2],
    )
    half_block = sub_rows // 2
    far_block = (sub_rows + half_block, vox_half)
    whole, up, down = call(
        functools.partial(centre_kernel, row_count, col_count, subjects),
        [sd((col_count * slice_rows, width)), sd(far_block, BF16), sd(far_block, BF16)],
        exchange(part, "row"),
        up1,
        down1,
        up2,
        down2,
    )
    weights = exchange(whole, "col")
    up3, down3 = ring_step(up, down, "row", row_count, 2)
    ring = [maps, up1, down1, up2, down2, up3, down3]
    places = [(k, 0, sub_rows, shift, 0) for k, shift in enumerate((0, -1, 1, -2, 2, -3, 3))]
    places += [(5, sub_rows, half_block, -4, 0), (6, sub_rows, half_block, 4, half_block)]
    group_shape = (groups, sub_rows, vox_half)
    whole_block = pl.BlockSpec(group_shape, lambda i: (0, 0, 0))
    col_kept, col_sent, sorted_blocks = pl.pallas_call(
        functools.partial(sort_kernel, places),
        grid=(1,),
        in_specs=[pl.BlockSpec(piece.shape, lambda i: (0, 0)) for piece in ring],
        out_specs=[whole_block, whole_block, pl.BlockSpec((8, 128), lambda i: (0, 0))],
        out_shape=[sd(group_shape, BF16), sd(group_shape, BF16), sd((8, 128))],
        compiler_params=ALL,
    )(*ring)

    half_rows = sub_rows // vox_count
    step = min(4 * sub_rows, block_rows)
    half_spec = pl.BlockSpec((step // sub_rows, half_rows, width), lambda i: (i, 0, 0))
    kept, sent, mean, centered = pl.pallas_call(
        functools.partial(sketch_kernel, col_count, vox_total),
        grid=(block_rows // step,),
        in_specs=[
            pl.BlockSpec((step, vox_half), lambda i: (i, 0)),
            pl.BlockSpec((col_count * slice_rows, width), lambda i: (0, 0)),
            pl.BlockSpec(memory_space=pl.ANY),
        ],
        out_specs=[
            half_spec,
            half_spec,
            pl.BlockSpec((1, vox_half), lambda i: (0, 0)),
            pl.BlockSpec((step, vox_half), lambda i: (i, 0)),
        ],
        scratch_shapes=[pltpu.VMEM((2, vox_half, width), BF16)],
        out_shape=[
            sd((col_count, half_rows, width)),
            sd((col_count, half_rows, width)),
            sd((1, vox_half)),
            sd((block_rows, vox_half), BF16),
        ],
        compiler_params=LARGE,
    )(row_maps, weights, sorted_blocks)
    got = lax.ppermute(sent, "vox", swap)
    cross_rows = width // col_count
    copies = row_count * vox_count
    slices, own, centered, col_sent = pl.pallas_call(
        functools.partial(cross_kernel, subjects, copies),
        grid=(1,),
        in_specs=[
            pl.BlockSpec((col_count, half_rows, width), lambda i: (0, 0, 0)),
            pl.BlockSpec((col_count, half_rows, width), lambda i: (0, 0, 0)),
            pl.BlockSpec(memory_space=pl.ANY),
            pl.BlockSpec(memory_space=pl.ANY),
        ],
        out_specs=[
            pl.BlockSpec((copies * cross_rows, width), lambda i: (0, 0)),
            pl.BlockSpec((half_rows, width), lambda i: (0, 0)),
            pl.BlockSpec(memory_space=pl.ANY),
            pl.BlockSpec(memory_space=pl.ANY),
        ],
        scratch_shapes=[pltpu.VMEM((width, width), F32)],
        out_shape=[
            sd((copies * cross_rows, width)),
            sd((half_rows, width)),
            sd((block_rows, vox_half), BF16),
            sd(group_shape, BF16),
        ],
        input_output_aliases={2: 2, 3: 3},
        compiler_params=LARGE,
    )(kept, got, centered, col_sent)
    other = lax.ppermute(centered, "vox", swap)
    col_other = lax.ppermute(col_sent, "vox", swap)
    means = jnp.concatenate([mean, lax.ppermute(mean, "vox", swap)], axis=0)
    own_cols = groups * sub_rows
    flat = (own_cols, vox_half)
    operands = (centered, other, col_kept.reshape(flat), col_other.reshape(flat), means)
    gram, first = gram_part(vox_total, groups, 0, None, *operands)
    (summed,) = call(
        functools.partial(sum_repeat_kernel, copies, col_count),
        [sd((width, width))],
        exchange(slices, ("row", "vox")),
        after=[first],
    )
    cross = exchange(summed, "col")
    gram, second = gram_part(vox_total, groups, 1, gram, *operands)
    factor, basis = call(
        functools.partial(cholesky_kernel, 16),
        [sd((width, width)), sd((half_rows, width))],
        cross,
        own,
        after=[second],
        scratch_shapes=[pltpu.VMEM((width, width + 128), F32)],
    )
    return gram.reshape(block_rows, groups, 1, sub_rows), basis, factor


def solution(mesh):
    placed = (P(("row", "col"), "vox"), P(("row", "col"), None))
    return jax.shard_map(
        shards,
        mesh=mesh,
        in_specs=placed,
        out_specs=(P("row", "vox", "col", None), P(("row", "col", "vox"), None), P()),
        check_vma=False,
    )
```

```python
import functools

import jax
import jax.numpy as jnp
from jax import lax
from jax.experimental import pallas as pl
from jax.experimental.pallas import tpu as pltpu
from jax.sharding import PartitionSpec as P

F32 = jnp.float32
BF16 = jnp.bfloat16
HIGHEST = lax.Precision.HIGHEST
PAD = 8
PARAMS = pltpu.CompilerParams(vmem_limit_bytes=24 * 1024 * 1024)
LARGE = pltpu.CompilerParams(vmem_limit_bytes=48 * 1024 * 1024)
SORT = pltpu.CompilerParams(vmem_limit_bytes=50 * 1024 * 1024)
ALL = pltpu.CompilerParams(vmem_limit_bytes=58 * 1024 * 1024)


def call(kernel, out_shape, *args, after=(), carry=(), params=PARAMS, **kw):
    count, outs = len(args), len(out_shape)
    others = len(after) + len(carry)

    def body(*refs):
        kernel(*refs[:count], *refs[count + others :][:outs], *refs[count + others + outs + len(carry) :])

    anywhere = pl.BlockSpec(memory_space=pl.ANY)
    vmem = pl.BlockSpec(memory_space=pltpu.VMEM)
    return pl.pallas_call(
        body,
        out_shape=[*out_shape, *[sd(x.shape, x.dtype) for x in carry]],
        in_specs=kw.pop("in_specs", [vmem] * count) + [anywhere] * others,
        out_specs=[vmem] * outs + [anywhere] * len(carry),
        input_output_aliases={count + len(after) + k: outs + k for k in range(len(carry))},
        compiler_params=params,
        **kw,
    )(*args, *after, *carry)


def sd(shape, dtype=F32):
    return jax.ShapeDtypeStruct(shape, dtype)


def project_kernel(pieces, maps_ref, probes_ref, out_ref, maps_in, probes_in, arrived):
    copies = [
        pltpu.make_async_copy(maps_ref, maps_in, arrived.at[0]),
        pltpu.make_async_copy(probes_ref, probes_in, arrived.at[1]),
    ]
    for copy in copies:
        copy.start()
    for copy in copies:
        copy.wait()
    maps = maps_in[...]
    probes = probes_in[...]
    vox, cols = maps.shape[1], probes.shape[1]
    width = vox // pieces
    sums = jnp.sum(maps.astype(F32), axis=0, keepdims=True)
    probe_sums = jnp.sum(probes.astype(F32), axis=0, keepdims=True)
    product = lax.dot_general(maps, probes, (((0,), (0,)), ((), ())), preferred_element_type=F32)
    for k in range(pieces):
        base = k * (width + PAD)
        out_ref[base : base + width, :] = product[k * width : (k + 1) * width, :]
        out_ref[base + width : base + width + 1, :width] = sums[:, k * width : (k + 1) * width]
        out_ref[base + width + 1 : base + width + 2, :] = probe_sums


def sum_repeat_kernel(sources, copies, in_ref, out_ref):
    rows = in_ref.shape[0] // sources
    total = in_ref[0:rows, :]
    for k in range(1, sources):
        total = total + in_ref[k * rows : (k + 1) * rows, :]
    for k in range(copies):
        out_ref[k * rows : (k + 1) * rows, :] = total


def centre_kernel(sources, copies, subjects, in_ref, out_ref):
    rows = in_ref.shape[0] // sources
    width = rows - PAD
    total = in_ref[0:rows, :]
    for k in range(1, sources):
        total = total + in_ref[k * rows : (k + 1) * rows, :]
    mean = total[width : width + 1, :width] / subjects
    probe_sums = total[width + 1 : width + 2, :]
    square = (width, width)
    on_diagonal = lax.broadcasted_iota(jnp.int32, square, 0) == lax.broadcasted_iota(
        jnp.int32, square, 1
    )
    mean_column = jnp.sum(jnp.where(on_diagonal, mean, 0.0), axis=1, keepdims=True)
    piece = total[:width, :] - mean_column * probe_sums
    for k in range(copies):
        out_ref[k * rows : k * rows + width, :] = piece
        out_ref[k * rows + width : k * rows + width + 1, :width] = mean


def split_terms(value, count=3):
    terms = []
    for _ in range(count):
        term = value.astype(BF16)
        terms.append(term)
        value = value - term.astype(F32)
    return terms


def sketch_kernel(
    pieces, vox_total, maps_ref, w_ref, _, kept_ref, sent_ref, mean_ref, centered_ref, parts
):
    rows = w_ref.shape[0] // pieces
    width = rows - PAD

    @pl.when(pl.program_id(0) == 0)
    def _():
        for k in range(pieces):
            w = w_ref[k * rows : k * rows + width, :] * (1.0 / vox_total)
            for n, part in enumerate(split_terms(w, 2)):
                parts[n, k * width : (k + 1) * width, :] = part
        mean_ref[...] = jnp.concatenate(
            [w_ref[k * rows + width : k * rows + width + 1, :width] for k in range(pieces)], axis=1
        )

    centered = (maps_ref[...].astype(F32) - mean_ref[...]).astype(BF16)
    centered_ref[...] = centered
    total = jnp.dot(centered, parts[0], preferred_element_type=F32)
    total += jnp.dot(centered, parts[1], preferred_element_type=F32)
    count, half = kept_ref.shape[0], kept_ref.shape[1]
    split = total.reshape(count, 2, half, total.shape[1])

    @pl.when(lax.axis_index("vox") == 0)
    def _():
        kept_ref[...] = split[:, 0]
        sent_ref[...] = split[:, 1]

    @pl.when(lax.axis_index("vox") == 1)
    def _():
        kept_ref[...] = split[:, 1]
        sent_ref[...] = split[:, 0]


def sort_kernel(places, *refs):
    pieces, (kept_ref, sent_ref, done_ref) = refs[:-3], refs[-3:]
    done_ref[...] = jnp.zeros(done_ref.shape, F32)
    groups = kept_ref.shape[0]
    total = 2 * groups
    for index, source, rows, shift, target in places:
        group = lax.rem(lax.axis_index("row") + (shift + total), total)
        mine = group // groups == lax.axis_index("vox")
        place = lax.rem(group, groups)
        piece = pieces[index]

        @pl.when(mine)
        def _(piece=piece, source=source, rows=rows, place=place, target=target):
            kept_ref[place, target : target + rows, :] = piece[source : source + rows, :]

        @pl.when(jnp.logical_not(mine))
        def _(piece=piece, source=source, rows=rows, place=place, target=target):
            sent_ref[place, target : target + rows, :] = piece[source : source + rows, :]


def cross_kernel(subjects, copies, kept_ref, got_ref, _, __, out_ref, own_ref, ___, ____, full):
    sketch = kept_ref[...] + got_ref[...]
    groups, half, cols = sketch.shape
    flat = sketch.reshape(groups * half, cols)
    full[...] = lax.dot_general(
        flat, flat, (((0,), (0,)), ((), ())), precision=HIGHEST, preferred_element_type=F32
    ) * (1.0 / subjects)
    col = lax.axis_index("col")
    rows = out_ref.shape[0] // copies
    piece = full[pl.ds(pl.multiple_of(col * rows, rows), rows), :]
    for k in range(copies):
        out_ref[k * rows : (k + 1) * rows, :] = piece
    own_ref[...] = kept_ref[col] + got_ref[col]


def cholesky_kernel(block, cross_ref, own_ref, factor_ref, basis_ref, work):
    size = cross_ref.shape[0]
    mine = own_ref.shape[0]
    work[:, :size] = cross_ref[...]
    padded = jnp.concatenate([own_ref[...], jnp.zeros((128 - mine, size), F32)], axis=0)
    work[:, size:] = padded.T
    shape = (block, 128)
    row_id = lax.broadcasted_iota(jnp.int32, shape, 0)

    def spread(value):
        return jnp.broadcast_to(value, shape)

    for start in range(0, size, block):
        lane0 = start // 128 * 128
        chunks = [work[start : start + block, k : k + 128] for k in range(lane0, size + 128, 128)]
        first = start - lane0
        columns = [spread(chunks[0][:, first + j : first + j + 1]) for j in range(block)]
        scale = jnp.zeros(shape, F32)
        for i in range(block):
            pivot = spread(columns[i][i : i + 1, :])
            scale = jnp.where(row_id == i, lax.rsqrt(pivot), scale)
            if i < block - 1:
                weight = jnp.where(row_id > i, columns[i] * (1.0 / pivot), 0.0)
                for j in range(i + 1, block):
                    columns[j] = columns[j] - weight * spread(columns[j][i : i + 1, :])
                chunks = [c - weight * spread(c[i : i + 1, :]) for c in chunks]
        panel = jnp.concatenate([c * scale for c in chunks], axis=1)
        work[start : start + block, lane0:] = panel
        stop = start + block
        if stop < size:
            lane1 = stop // 128 * 128
            right = split_terms(panel[:, lane1 - lane0 :])
            left = [part[:, : size - lane1] for part in right]
            update = lax.dot_general(
                jnp.concatenate([left[k] for k in (0, 0, 1, 0, 2, 1)], axis=0),
                jnp.concatenate([right[k] for k in (0, 1, 0, 2, 0, 1)], axis=0),
                (((0,), (0,)), ((), ())),
                preferred_element_type=F32,
            )
            work[stop:, lane1:] = work[stop:, lane1:] - update[stop - lane1 :, :]
    square = (size, size)
    upper = lax.broadcasted_iota(jnp.int32, square, 0) <= lax.broadcasted_iota(jnp.int32, square, 1)
    factor_ref[...] = jnp.where(upper, work[:, :size], 0.0)
    basis_ref[...] = work[:, size:].T[:mine, :]


def gram_kernel(vox_total, own_ref, other_ref, col_own_ref, col_other_ref, means_ref, _, out_ref, done_ref, cols):
    half = own_ref.shape[1]

    @pl.when(pl.program_id(0) == 0)
    def _():
        for k, ref in enumerate((col_own_ref, col_other_ref)):
            mean = means_ref[k : k + 1, :]
            cols[:, k * half : (k + 1) * half] = (ref[...].astype(F32) - mean).astype(BF16)

    contract = (((1,), (1,)), ((), ()))
    tile = lax.dot_general(own_ref[...], cols[:, :half], contract, preferred_element_type=F32)
    tile += lax.dot_general(other_ref[...], cols[:, half:], contract, preferred_element_type=F32)
    tile = tile * (1.0 / vox_total)
    done_ref[...] = jnp.zeros(done_ref.shape, F32)
    rows = tile.shape[0]
    groups = tile.shape[1] // 128
    for a in range(groups):
        out_ref[pl.ds(a, rows, stride=groups), :] = tile[:, a * 128 : (a + 1) * 128]


def gram_part(vox_total, groups, part, before, own, other, col_own, col_other, means):
    rows, vox_half = own.shape
    tall = min(512, rows // 2)
    steps = rows // tall // 2
    row_spec = pl.BlockSpec((tall, vox_half), lambda i: (i + part * steps, 0))
    col_spec = pl.BlockSpec(col_own.shape, lambda i: (0, 0))
    return pl.pallas_call(
        functools.partial(gram_kernel, vox_total),
        grid=(steps,),
        in_specs=[
            row_spec,
            row_spec,
            col_spec,
            col_spec,
            pl.BlockSpec(means.shape, lambda i: (0, 0)),
            pl.BlockSpec(memory_space=pl.ANY),
        ],
        out_specs=[
            pl.BlockSpec((tall * groups, 128), lambda i: (i + part * steps, 0)),
            pl.BlockSpec((8, 128), lambda i: (0, 0)),
        ],
        out_shape=[sd((rows * groups, 128)), sd((8, 128))],
        scratch_shapes=[pltpu.VMEM((col_own.shape[0], vox_total), BF16)],
        input_output_aliases={} if before is None else {5: 0},
        compiler_params=LARGE,
    )(own, other, col_own, col_other, means, means if before is None else before)


def ring_step(up, down, axis, size, hops=1):
    ahead = [(i, (i + hops) % size) for i in range(size)]
    back = [(i, (i - hops) % size) for i in range(size)]
    return lax.ppermute(up, axis, ahead), lax.ppermute(down, axis, back)


def shards(maps, probes):
    sub_rows, vox_half = maps.shape
    width = probes.shape[1]
    row_count = lax.axis_size("row")
    col_count = lax.axis_size("col")
    vox_count = lax.axis_size("vox")
    subjects = sub_rows * row_count * col_count
    vox_total = vox_half * vox_count
    block_rows = sub_rows * col_count
    groups = row_count // vox_count
    swap = [(0, 1), (1, 0)]

    def exchange(value, axis):
        return lax.all_to_all(value, axis, 0, 0, tiled=True)

    row_maps = lax.all_gather(maps, "col", axis=0, tiled=True)
    slice_rows = vox_half // col_count + PAD
    up1, down1 = ring_step(maps, maps, "row", row_count)
    up2, down2 = ring_step(up1, down1, "row", row_count)
    (local,) = call(
        functools.partial(project_kernel, col_count),
        [sd((col_count * slice_rows, width))],
        maps,
        probes,
        in_specs=[pl.BlockSpec(memory_space=pl.ANY)] * 2,
        params=ALL,
        scratch_shapes=[
            pltpu.VMEM(maps.shape, BF16),
            pltpu.VMEM(probes.shape, BF16),
            pltpu.SemaphoreType.DMA((2,)),
        ],
    )
    (part,) = call(
        functools.partial(sum_repeat_kernel, col_count, row_count),
        [sd((row_count * slice_rows, width))],
        exchange(local, "col"),
        after=[up1, down1, up2, down2],
    )
    half_block = sub_rows // 2
    whole, up2, down2 = call(
        functools.partial(centre_kernel, row_count, col_count, subjects),
        [sd((col_count * slice_rows, width))],
        exchange(part, "row"),
        carry=[up2, down2],
    )
    weights = exchange(whole, "col")
    up3, down3 = ring_step(up2, down2, "row", row_count)
    up4, down4 = ring_step(up2[:half_block], down2[half_block:], "row", row_count, 2)
    ring = [maps, up1, down1, up2, down2, up3, down3, up4, down4]
    places = [(k, 0, sub_rows, shift, 0) for k, shift in enumerate((0, -1, 1, -2, 2, -3, 3))]
    places += [(7, 0, half_block, -4, 0), (8, 0, half_block, 4, half_block)]
    group_shape = (groups, sub_rows, vox_half)
    whole_block = pl.BlockSpec(group_shape, lambda i: (0, 0, 0))
    col_kept, col_sent, sorted_blocks = pl.pallas_call(
        functools.partial(sort_kernel, places),
        grid=(1,),
        in_specs=[pl.BlockSpec(piece.shape, lambda i: (0, 0)) for piece in ring],
        out_specs=[whole_block, whole_block, pl.BlockSpec((8, 128), lambda i: (0, 0))],
        out_shape=[sd(group_shape, BF16), sd(group_shape, BF16), sd((8, 128))],
        compiler_params=SORT,
    )(*ring)

    half_rows = sub_rows // vox_count
    step = min(4 * sub_rows, block_rows)
    half_spec = pl.BlockSpec((step // sub_rows, half_rows, width), lambda i: (i, 0, 0))
    kept, sent, mean, centered = pl.pallas_call(
        functools.partial(sketch_kernel, col_count, vox_total),
        grid=(block_rows // step,),
        in_specs=[
            pl.BlockSpec((step, vox_half), lambda i: (i, 0)),
            pl.BlockSpec((col_count * slice_rows, width), lambda i: (0, 0)),
            pl.BlockSpec(memory_space=pl.ANY),
        ],
        out_specs=[
            half_spec,
            half_spec,
            pl.BlockSpec((1, vox_half), lambda i: (0, 0)),
            pl.BlockSpec((step, vox_half), lambda i: (i, 0)),
        ],
        scratch_shapes=[pltpu.VMEM((2, vox_half, width), BF16)],
        out_shape=[
            sd((col_count, half_rows, width)),
            sd((col_count, half_rows, width)),
            sd((1, vox_half)),
            sd((block_rows, vox_half), BF16),
        ],
        compiler_params=LARGE,
    )(row_maps, weights, sorted_blocks)
    got = lax.ppermute(sent, "vox", swap)
    cross_rows = width // col_count
    copies = row_count * vox_count
    slices, own, centered, col_sent = pl.pallas_call(
        functools.partial(cross_kernel, subjects, copies),
        grid=(1,),
        in_specs=[
            pl.BlockSpec((col_count, half_rows, width), lambda i: (0, 0, 0)),
            pl.BlockSpec((col_count, half_rows, width), lambda i: (0, 0, 0)),
            pl.BlockSpec(memory_space=pl.ANY),
            pl.BlockSpec(memory_space=pl.ANY),
        ],
        out_specs=[
            pl.BlockSpec((copies * cross_rows, width), lambda i: (0, 0)),
            pl.BlockSpec((half_rows, width), lambda i: (0, 0)),
            pl.BlockSpec(memory_space=pl.ANY),
            pl.BlockSpec(memory_space=pl.ANY),
        ],
        scratch_shapes=[pltpu.VMEM((width, width), F32)],
        out_shape=[
            sd((copies * cross_rows, width)),
            sd((half_rows, width)),
            sd((block_rows, vox_half), BF16),
            sd(group_shape, BF16),
        ],
        input_output_aliases={2: 2, 3: 3},
        compiler_params=LARGE,
    )(kept, got, centered, col_sent)
    other = lax.ppermute(centered, "vox", swap)
    col_other = lax.ppermute(col_sent, "vox", swap)
    means = jnp.concatenate([mean, lax.ppermute(mean, "vox", swap)], axis=0)
    own_cols = groups * sub_rows
    flat = (own_cols, vox_half)
    operands = (centered, other, col_kept.reshape(flat), col_other.reshape(flat), means)
    gram, first = gram_part(vox_total, groups, 0, None, *operands)
    (summed,) = call(
        functools.partial(sum_repeat_kernel, copies, col_count),
        [sd((width, width))],
        exchange(slices, ("row", "vox")),
        after=[first],
    )
    cross = exchange(summed, "col")
    gram, second = gram_part(vox_total, groups, 1, gram, *operands)
    factor, basis = call(
        functools.partial(cholesky_kernel, 16),
        [sd((width, width)), sd((half_rows, width))],
        cross,
        own,
        after=[second],
        scratch_shapes=[pltpu.VMEM((width, width + 128), F32)],
    )
    return gram.reshape(block_rows, groups, 1, sub_rows), basis, factor


def solution(mesh):
    placed = (P(("row", "col"), "vox"), P(("row", "col"), None))
    return jax.shard_map(
        shards,
        mesh=mesh,
        in_specs=placed,
        out_specs=(P("row", "vox", "col", None), P(("row", "col", "vox"), None), P()),
        check_vma=False,
    )
```

```python
import functools

import jax
import jax.numpy as jnp
from jax import lax
from jax.experimental import pallas as pl
from jax.experimental.pallas import tpu as pltpu
from jax.sharding import PartitionSpec as P

F32 = jnp.float32
BF16 = jnp.bfloat16
HIGHEST = lax.Precision.HIGHEST
PAD = 8
PARAMS = pltpu.CompilerParams(vmem_limit_bytes=24 * 1024 * 1024)
LARGE = pltpu.CompilerParams(vmem_limit_bytes=48 * 1024 * 1024)
SORT = pltpu.CompilerParams(vmem_limit_bytes=50 * 1024 * 1024)
ALL = pltpu.CompilerParams(vmem_limit_bytes=58 * 1024 * 1024)


def call(kernel, out_shape, *args, after=(), carry=(), params=PARAMS, **kw):
    count, outs = len(args), len(out_shape)
    others = len(after) + len(carry)

    def body(*refs):
        kernel(*refs[:count], *refs[count + others :][:outs], *refs[count + others + outs + len(carry) :])

    anywhere = pl.BlockSpec(memory_space=pl.ANY)
    vmem = pl.BlockSpec(memory_space=pltpu.VMEM)
    return pl.pallas_call(
        body,
        out_shape=[*out_shape, *[sd(x.shape, x.dtype) for x in carry]],
        in_specs=kw.pop("in_specs", [vmem] * count) + [anywhere] * others,
        out_specs=[vmem] * outs + [anywhere] * len(carry),
        input_output_aliases={count + len(after) + k: outs + k for k in range(len(carry))},
        compiler_params=params,
        **kw,
    )(*args, *after, *carry)


def sd(shape, dtype=F32):
    return jax.ShapeDtypeStruct(shape, dtype)


def project_kernel(pieces, maps_ref, probes_ref, out_ref, maps_in, probes_in, arrived):
    copies = [
        pltpu.make_async_copy(maps_ref, maps_in, arrived.at[0]),
        pltpu.make_async_copy(probes_ref, probes_in, arrived.at[1]),
    ]
    for copy in copies:
        copy.start()
    for copy in copies:
        copy.wait()
    maps = maps_in[...]
    probes = probes_in[...]
    vox, cols = maps.shape[1], probes.shape[1]
    width = vox // pieces
    sums = jnp.sum(maps.astype(F32), axis=0, keepdims=True)
    probe_sums = jnp.sum(probes.astype(F32), axis=0, keepdims=True)
    product = lax.dot_general(maps, probes, (((0,), (0,)), ((), ())), preferred_element_type=F32)
    for k in range(pieces):
        base = k * (width + PAD)
        out_ref[base : base + width, :] = product[k * width : (k + 1) * width, :]
        out_ref[base + width : base + width + 1, :width] = sums[:, k * width : (k + 1) * width]
        out_ref[base + width + 1 : base + width + 2, :] = probe_sums


def sum_repeat_kernel(sources, copies, in_ref, out_ref):
    rows = in_ref.shape[0] // sources
    total = in_ref[0:rows, :]
    for k in range(1, sources):
        total = total + in_ref[k * rows : (k + 1) * rows, :]
    for k in range(copies):
        out_ref[k * rows : (k + 1) * rows, :] = total


def centre_kernel(sources, copies, subjects, in_ref, out_ref):
    rows = in_ref.shape[0] // sources
    width = rows - PAD
    total = in_ref[0:rows, :]
    for k in range(1, sources):
        total = total + in_ref[k * rows : (k + 1) * rows, :]
    mean = total[width : width + 1, :width] / subjects
    probe_sums = total[width + 1 : width + 2, :]
    square = (width, width)
    on_diagonal = lax.broadcasted_iota(jnp.int32, square, 0) == lax.broadcasted_iota(
        jnp.int32, square, 1
    )
    mean_column = jnp.sum(jnp.where(on_diagonal, mean, 0.0), axis=1, keepdims=True)
    piece = total[:width, :] - mean_column * probe_sums
    for k in range(copies):
        out_ref[k * rows : k * rows + width, :] = piece
        out_ref[k * rows + width : k * rows + width + 1, :width] = mean


def split_terms(value, count=3):
    terms = []
    for _ in range(count):
        term = value.astype(BF16)
        terms.append(term)
        value = value - term.astype(F32)
    return terms


def sketch_kernel(
    pieces, vox_total, maps_ref, w_ref, _, kept_ref, sent_ref, mean_ref, centered_ref, parts
):
    rows = w_ref.shape[0] // pieces
    width = rows - PAD

    @pl.when(pl.program_id(0) == 0)
    def _():
        for k in range(pieces):
            w = w_ref[k * rows : k * rows + width, :] * (1.0 / vox_total)
            for n, part in enumerate(split_terms(w, 2)):
                parts[n, k * width : (k + 1) * width, :] = part
        mean_ref[...] = jnp.concatenate(
            [w_ref[k * rows + width : k * rows + width + 1, :width] for k in range(pieces)], axis=1
        )

    centered = (maps_ref[...].astype(F32) - mean_ref[...]).astype(BF16)
    centered_ref[...] = centered
    total = jnp.dot(centered, parts[0], preferred_element_type=F32)
    total += jnp.dot(centered, parts[1], preferred_element_type=F32)
    count, half = kept_ref.shape[0], kept_ref.shape[1]
    split = total.reshape(count, 2, half, total.shape[1])

    @pl.when(lax.axis_index("vox") == 0)
    def _():
        kept_ref[...] = split[:, 0]
        sent_ref[...] = split[:, 1]

    @pl.when(lax.axis_index("vox") == 1)
    def _():
        kept_ref[...] = split[:, 1]
        sent_ref[...] = split[:, 0]


def sort_kernel(places, *refs):
    pieces, (kept_ref, sent_ref, done_ref) = refs[:-3], refs[-3:]
    done_ref[...] = jnp.zeros(done_ref.shape, F32)
    groups = kept_ref.shape[0]
    total = 2 * groups
    for index, source, rows, shift, target in places:
        group = lax.rem(lax.axis_index("row") + (shift + total), total)
        mine = group // groups == lax.axis_index("vox")
        place = lax.rem(group, groups)
        piece = pieces[index]

        @pl.when(mine)
        def _(piece=piece, source=source, rows=rows, place=place, target=target):
            kept_ref[place, target : target + rows, :] = piece[source : source + rows, :]

        @pl.when(jnp.logical_not(mine))
        def _(piece=piece, source=source, rows=rows, place=place, target=target):
            sent_ref[place, target : target + rows, :] = piece[source : source + rows, :]


def cross_kernel(subjects, kept_ref, got_ref, mean_ref, _, __, out_ref, own_ref, ___, ____, full):
    sketch = kept_ref[...] + got_ref[...]
    groups, half, cols = sketch.shape
    flat = sketch.reshape(groups * half, cols)
    full[...] = lax.dot_general(
        flat, flat, (((0,), (0,)), ((), ())), precision=HIGHEST, preferred_element_type=F32
    ) * (1.0 / subjects)
    col = lax.axis_index("col")
    rows = out_ref.shape[0] - PAD
    out_ref[:rows, :] = full[pl.ds(pl.multiple_of(col * rows, rows), rows), :]
    out_ref[rows:, :] = jnp.zeros((PAD, cols), F32)
    for k in range(mean_ref.shape[1] // cols):
        out_ref[rows + k : rows + k + 1, :] = mean_ref[:, k * cols : (k + 1) * cols]
    own_ref[...] = kept_ref[col] + got_ref[col]


def pair_kernel(copies, mine_ref, got_ref, out_ref, means_ref):
    rows = mine_ref.shape[0] - PAD
    cols = mine_ref.shape[1]
    total = mine_ref[:rows, :] + got_ref[:rows, :]
    for k in range(copies):
        out_ref[k * rows : (k + 1) * rows, :] = total
    for n, ref in enumerate((mine_ref, got_ref)):
        for k in range(means_ref.shape[1] // cols):
            row = ref[rows + k : rows + k + 1, :]
            means_ref[n : n + 1, k * cols : (k + 1) * cols] = row


def cholesky_kernel(block, cross_ref, own_ref, factor_ref, basis_ref, work):
    size = cross_ref.shape[0]
    mine = own_ref.shape[0]
    work[:, :size] = cross_ref[...]
    padded = jnp.concatenate([own_ref[...], jnp.zeros((128 - mine, size), F32)], axis=0)
    work[:, size:] = padded.T
    shape = (block, 128)
    row_id = lax.broadcasted_iota(jnp.int32, shape, 0)

    def spread(value):
        return jnp.broadcast_to(value, shape)

    for start in range(0, size, block):
        lane0 = start // 128 * 128
        chunks = [work[start : start + block, k : k + 128] for k in range(lane0, size + 128, 128)]
        first = start - lane0
        columns = [spread(chunks[0][:, first + j : first + j + 1]) for j in range(block)]
        scale = jnp.zeros(shape, F32)
        for i in range(block):
            pivot = spread(columns[i][i : i + 1, :])
            scale = jnp.where(row_id == i, lax.rsqrt(pivot), scale)
            if i < block - 1:
                weight = jnp.where(row_id > i, columns[i] * (1.0 / pivot), 0.0)
                for j in range(i + 1, block):
                    columns[j] = columns[j] - weight * spread(columns[j][i : i + 1, :])
                chunks = [c - weight * spread(c[i : i + 1, :]) for c in chunks]
        panel = jnp.concatenate([c * scale for c in chunks], axis=1)
        work[start : start + block, lane0:] = panel
        stop = start + block
        if stop < size:
            lane1 = stop // 128 * 128
            right = split_terms(panel[:, lane1 - lane0 :])
            left = [part[:, : size - lane1] for part in right]
            update = lax.dot_general(
                jnp.concatenate([left[k] for k in (0, 0, 1, 0, 2, 1)], axis=0),
                jnp.concatenate([right[k] for k in (0, 1, 0, 2, 0, 1)], axis=0),
                (((0,), (0,)), ((), ())),
                preferred_element_type=F32,
            )
            work[stop:, lane1:] = work[stop:, lane1:] - update[stop - lane1 :, :]
    square = (size, size)
    upper = lax.broadcasted_iota(jnp.int32, square, 0) <= lax.broadcasted_iota(jnp.int32, square, 1)
    factor_ref[...] = jnp.where(upper, work[:, :size], 0.0)
    basis_ref[...] = work[:, size:].T[:mine, :]


def gram_kernel(vox_total, own_ref, other_ref, col_own_ref, col_other_ref, means_ref, _, out_ref, done_ref, cols):
    half = own_ref.shape[1]

    @pl.when(pl.program_id(0) == 0)
    def _():
        for k, ref in enumerate((col_own_ref, col_other_ref)):
            mean = means_ref[k : k + 1, :]
            cols[:, k * half : (k + 1) * half] = (ref[...].astype(F32) - mean).astype(BF16)

    contract = (((1,), (1,)), ((), ()))
    tile = lax.dot_general(own_ref[...], cols[:, :half], contract, preferred_element_type=F32)
    tile += lax.dot_general(other_ref[...], cols[:, half:], contract, preferred_element_type=F32)
    tile = tile * (1.0 / vox_total)
    done_ref[...] = jnp.zeros(done_ref.shape, F32)
    rows = tile.shape[0]
    groups = tile.shape[1] // 128
    for a in range(groups):
        out_ref[pl.ds(a, rows, stride=groups), :] = tile[:, a * 128 : (a + 1) * 128]


def gram_part(vox_total, groups, part, before, own, other, col_own, col_other, means):
    rows, vox_half = own.shape
    tall = min(512, rows // 2)
    steps = rows // tall // 2
    row_spec = pl.BlockSpec((tall, vox_half), lambda i: (i + part * steps, 0))
    col_spec = pl.BlockSpec(col_own.shape, lambda i: (0, 0))
    return pl.pallas_call(
        functools.partial(gram_kernel, vox_total),
        grid=(steps,),
        in_specs=[
            row_spec,
            row_spec,
            col_spec,
            col_spec,
            pl.BlockSpec(means.shape, lambda i: (0, 0)),
            pl.BlockSpec(memory_space=pl.ANY),
        ],
        out_specs=[
            pl.BlockSpec((tall * groups, 128), lambda i: (i + part * steps, 0)),
            pl.BlockSpec((8, 128), lambda i: (0, 0)),
        ],
        out_shape=[sd((rows * groups, 128)), sd((8, 128))],
        scratch_shapes=[pltpu.VMEM((col_own.shape[0], vox_total), BF16)],
        input_output_aliases={} if before is None else {5: 0},
        compiler_params=LARGE,
    )(own, other, col_own, col_other, means, means if before is None else before)


def ring_step(up, down, axis, size, hops=1):
    ahead = [(i, (i + hops) % size) for i in range(size)]
    back = [(i, (i - hops) % size) for i in range(size)]
    return lax.ppermute(up, axis, ahead), lax.ppermute(down, axis, back)


def shards(maps, probes):
    sub_rows, vox_half = maps.shape
    width = probes.shape[1]
    row_count = lax.axis_size("row")
    col_count = lax.axis_size("col")
    vox_count = lax.axis_size("vox")
    subjects = sub_rows * row_count * col_count
    vox_total = vox_half * vox_count
    block_rows = sub_rows * col_count
    groups = row_count // vox_count
    swap = [(0, 1), (1, 0)]

    def exchange(value, axis):
        return lax.all_to_all(value, axis, 0, 0, tiled=True)

    row_maps = lax.all_gather(maps, "col", axis=0, tiled=True)
    slice_rows = vox_half // col_count + PAD
    up1, down1 = ring_step(maps, maps, "row", row_count)
    up2, down2 = ring_step(up1, down1, "row", row_count)
    (local,) = call(
        functools.partial(project_kernel, col_count),
        [sd((col_count * slice_rows, width))],
        maps,
        probes,
        in_specs=[pl.BlockSpec(memory_space=pl.ANY)] * 2,
        params=ALL,
        scratch_shapes=[
            pltpu.VMEM(maps.shape, BF16),
            pltpu.VMEM(probes.shape, BF16),
            pltpu.SemaphoreType.DMA((2,)),
        ],
    )
    (part,) = call(
        functools.partial(sum_repeat_kernel, col_count, row_count),
        [sd((row_count * slice_rows, width))],
        exchange(local, "col"),
        after=[up1, down1, up2, down2],
    )
    half_block = sub_rows // 2
    whole, up2, down2 = call(
        functools.partial(centre_kernel, row_count, col_count, subjects),
        [sd((col_count * slice_rows, width))],
        exchange(part, "row"),
        carry=[up2, down2],
    )
    weights = exchange(whole, "col")
    up3, down3 = ring_step(up2, down2, "row", row_count)
    up4, down4 = ring_step(up2[:half_block], down2[half_block:], "row", row_count, 2)
    ring = [maps, up1, down1, up2, down2, up3, down3, up4, down4]
    places = [(k, 0, sub_rows, shift, 0) for k, shift in enumerate((0, -1, 1, -2, 2, -3, 3))]
    places += [(7, 0, half_block, -4, 0), (8, 0, half_block, 4, half_block)]
    group_shape = (groups, sub_rows, vox_half)
    whole_block = pl.BlockSpec(group_shape, lambda i: (0, 0, 0))
    col_kept, col_sent, sorted_blocks = pl.pallas_call(
        functools.partial(sort_kernel, places),
        grid=(1,),
        in_specs=[pl.BlockSpec(piece.shape, lambda i: (0, 0)) for piece in ring],
        out_specs=[whole_block, whole_block, pl.BlockSpec((8, 128), lambda i: (0, 0))],
        out_shape=[sd(group_shape, BF16), sd(group_shape, BF16), sd((8, 128))],
        compiler_params=SORT,
    )(*ring)

    half_rows = sub_rows // vox_count
    step = min(4 * sub_rows, block_rows)
    half_spec = pl.BlockSpec((step // sub_rows, half_rows, width), lambda i: (i, 0, 0))
    kept, sent, mean, centered = pl.pallas_call(
        functools.partial(sketch_kernel, col_count, vox_total),
        grid=(block_rows // step,),
        in_specs=[
            pl.BlockSpec((step, vox_half), lambda i: (i, 0)),
            pl.BlockSpec((col_count * slice_rows, width), lambda i: (0, 0)),
            pl.BlockSpec(memory_space=pl.ANY),
        ],
        out_specs=[
            half_spec,
            half_spec,
            pl.BlockSpec((1, vox_half), lambda i: (0, 0)),
            pl.BlockSpec((step, vox_half), lambda i: (i, 0)),
        ],
        scratch_shapes=[pltpu.VMEM((2, vox_half, width), BF16)],
        out_shape=[
            sd((col_count, half_rows, width)),
            sd((col_count, half_rows, width)),
            sd((1, vox_half)),
            sd((block_rows, vox_half), BF16),
        ],
        compiler_params=LARGE,
    )(row_maps, weights, sorted_blocks)
    got = lax.ppermute(sent, "vox", swap)
    cross_rows = width // col_count
    slice_shape = (cross_rows + PAD, width)
    slices, own, centered, col_sent = pl.pallas_call(
        functools.partial(cross_kernel, subjects),
        grid=(1,),
        in_specs=[
            pl.BlockSpec((col_count, half_rows, width), lambda i: (0, 0, 0)),
            pl.BlockSpec((col_count, half_rows, width), lambda i: (0, 0, 0)),
            pl.BlockSpec((1, vox_half), lambda i: (0, 0)),
            pl.BlockSpec(memory_space=pl.ANY),
            pl.BlockSpec(memory_space=pl.ANY),
        ],
        out_specs=[
            pl.BlockSpec(slice_shape, lambda i: (0, 0)),
            pl.BlockSpec((half_rows, width), lambda i: (0, 0)),
            pl.BlockSpec(memory_space=pl.ANY),
            pl.BlockSpec(memory_space=pl.ANY),
        ],
        scratch_shapes=[pltpu.VMEM((width, width), F32)],
        out_shape=[
            sd(slice_shape),
            sd((half_rows, width)),
            sd((block_rows, vox_half), BF16),
            sd(group_shape, BF16),
        ],
        input_output_aliases={3: 2, 4: 3},
        compiler_params=LARGE,
    )(kept, got, mean, centered, col_sent)
    shared, means = call(
        functools.partial(pair_kernel, row_count),
        [sd((row_count * cross_rows, width)), sd((vox_count, vox_half))],
        slices,
        lax.ppermute(slices, "vox", swap),
    )

    other = lax.ppermute(centered, "vox", swap)
    col_other = lax.ppermute(col_sent, "vox", swap)
    own_cols = groups * sub_rows
    flat = (own_cols, vox_half)
    operands = (centered, other, col_kept.reshape(flat), col_other.reshape(flat), means)
    gram, first = gram_part(vox_total, groups, 0, None, *operands)
    (summed,) = call(
        functools.partial(sum_repeat_kernel, row_count, col_count),
        [sd((width, width))],
        exchange(shared, "row"),
        after=[first],
    )
    cross = exchange(summed, "col")
    gram, second = gram_part(vox_total, groups, 1, gram, *operands)
    factor, basis = call(
        functools.partial(cholesky_kernel, 16),
        [sd((width, width)), sd((half_rows, width))],
        cross,
        own,
        after=[second],
        scratch_shapes=[pltpu.VMEM((width, width + 128), F32)],
    )
    return gram.reshape(block_rows, groups, 1, sub_rows), basis, factor


def solution(mesh):
    placed = (P(("row", "col"), "vox"), P(("row", "col"), None))
    return jax.shard_map(
        shards,
        mesh=mesh,
        in_specs=placed,
        out_specs=(P("row", "vox", "col", None), P(("row", "col", "vox"), None), P()),
        check_vma=False,
    )
```

```python
import functools

import jax
import jax.numpy as jnp
from jax import lax
from jax.experimental import pallas as pl
from jax.experimental.pallas import tpu as pltpu
from jax.sharding import PartitionSpec as P

F32 = jnp.float32
BF16 = jnp.bfloat16
HIGHEST = lax.Precision.HIGHEST
PAD = 8
PARAMS = pltpu.CompilerParams(vmem_limit_bytes=24 * 1024 * 1024)
LARGE = pltpu.CompilerParams(vmem_limit_bytes=48 * 1024 * 1024)
SORT = pltpu.CompilerParams(vmem_limit_bytes=50 * 1024 * 1024)
ALL = pltpu.CompilerParams(vmem_limit_bytes=58 * 1024 * 1024)


def call(kernel, out_shape, *args, after=(), carry=(), params=PARAMS, **kw):
    count, outs = len(args), len(out_shape)
    others = len(after) + len(carry)

    def body(*refs):
        kernel(*refs[:count], *refs[count + others :][:outs], *refs[count + others + outs + len(carry) :])

    anywhere = pl.BlockSpec(memory_space=pl.ANY)
    vmem = pl.BlockSpec(memory_space=pltpu.VMEM)
    return pl.pallas_call(
        body,
        out_shape=[*out_shape, *[sd(x.shape, x.dtype) for x in carry]],
        in_specs=kw.pop("in_specs", [vmem] * count) + [anywhere] * others,
        out_specs=[vmem] * outs + [anywhere] * len(carry),
        input_output_aliases={count + len(after) + k: outs + k for k in range(len(carry))},
        compiler_params=params,
        **kw,
    )(*args, *after, *carry)


def sd(shape, dtype=F32):
    return jax.ShapeDtypeStruct(shape, dtype)


def project_kernel(pieces, maps_ref, probes_ref, out_ref, maps_in, probes_in, arrived):
    copies = [
        pltpu.make_async_copy(maps_ref, maps_in, arrived.at[0]),
        pltpu.make_async_copy(probes_ref, probes_in, arrived.at[1]),
    ]
    for copy in copies:
        copy.start()
    for copy in copies:
        copy.wait()
    maps = maps_in[...]
    probes = probes_in[...]
    vox, cols = maps.shape[1], probes.shape[1]
    width = vox // pieces
    sums = jnp.sum(maps.astype(F32), axis=0, keepdims=True)
    probe_sums = jnp.sum(probes.astype(F32), axis=0, keepdims=True)
    product = lax.dot_general(maps, probes, (((0,), (0,)), ((), ())), preferred_element_type=F32)
    for k in range(pieces):
        base = k * (width + PAD)
        out_ref[base : base + width, :] = product[k * width : (k + 1) * width, :]
        out_ref[base + width : base + width + 1, :width] = sums[:, k * width : (k + 1) * width]
        out_ref[base + width + 1 : base + width + 2, :] = probe_sums


def sum_repeat_kernel(sources, copies, in_ref, out_ref):
    rows = in_ref.shape[0] // sources
    total = in_ref[0:rows, :]
    for k in range(1, sources):
        total = total + in_ref[k * rows : (k + 1) * rows, :]
    for k in range(copies):
        out_ref[k * rows : (k + 1) * rows, :] = total


def centre_kernel(sources, copies, subjects, in_ref, out_ref):
    rows = in_ref.shape[0] // sources
    width = rows - PAD
    total = in_ref[0:rows, :]
    for k in range(1, sources):
        total = total + in_ref[k * rows : (k + 1) * rows, :]
    mean = total[width : width + 1, :width] / subjects
    probe_sums = total[width + 1 : width + 2, :]
    square = (width, width)
    on_diagonal = lax.broadcasted_iota(jnp.int32, square, 0) == lax.broadcasted_iota(
        jnp.int32, square, 1
    )
    mean_column = jnp.sum(jnp.where(on_diagonal, mean, 0.0), axis=1, keepdims=True)
    piece = total[:width, :] - mean_column * probe_sums
    for k in range(copies):
        out_ref[k * rows : k * rows + width, :] = piece
        out_ref[k * rows + width : k * rows + width + 1, :width] = mean


def split_terms(value, count=3):
    terms = []
    for _ in range(count):
        term = value.astype(BF16)
        terms.append(term)
        value = value - term.astype(F32)
    return terms


def sketch_kernel(
    pieces, vox_total, maps_ref, w_ref, _, kept_ref, sent_ref, mean_ref, centered_ref, parts
):
    rows = w_ref.shape[0] // pieces
    width = rows - PAD

    @pl.when(pl.program_id(0) == 0)
    def _():
        for k in range(pieces):
            w = w_ref[k * rows : k * rows + width, :] * (1.0 / vox_total)
            for n, part in enumerate(split_terms(w, 2)):
                parts[n, k * width : (k + 1) * width, :] = part
        mean_ref[...] = jnp.concatenate(
            [w_ref[k * rows + width : k * rows + width + 1, :width] for k in range(pieces)], axis=1
        )

    centered = (maps_ref[...].astype(F32) - mean_ref[...]).astype(BF16)
    centered_ref[...] = centered
    total = jnp.dot(centered, parts[0], preferred_element_type=F32)
    total += jnp.dot(centered, parts[1], preferred_element_type=F32)
    count, half = kept_ref.shape[0], kept_ref.shape[1]
    split = total.reshape(count, 2, half, total.shape[1])

    @pl.when(lax.axis_index("vox") == 0)
    def _():
        kept_ref[...] = split[:, 0]
        sent_ref[...] = split[:, 1]

    @pl.when(lax.axis_index("vox") == 1)
    def _():
        kept_ref[...] = split[:, 1]
        sent_ref[...] = split[:, 0]


def sort_kernel(places, *refs):
    pieces, (kept_ref, sent_ref, done_ref) = refs[:-3], refs[-3:]
    done_ref[...] = jnp.zeros(done_ref.shape, F32)
    groups = kept_ref.shape[0]
    total = 2 * groups
    for index, source, rows, shift, target in places:
        group = lax.rem(lax.axis_index("row") + (shift + total), total)
        mine = group // groups == lax.axis_index("vox")
        place = lax.rem(group, groups)
        piece = pieces[index]

        @pl.when(mine)
        def _(piece=piece, source=source, rows=rows, place=place, target=target):
            kept_ref[place, target : target + rows, :] = piece[source : source + rows, :]

        @pl.when(jnp.logical_not(mine))
        def _(piece=piece, source=source, rows=rows, place=place, target=target):
            sent_ref[place, target : target + rows, :] = piece[source : source + rows, :]


def cross_kernel(subjects, kept_ref, got_ref, mean_ref, out_ref, own_ref, full):
    sketch = kept_ref[...] + got_ref[...]
    groups, half, cols = sketch.shape
    flat = sketch.reshape(groups * half, cols)
    full[...] = lax.dot_general(
        flat, flat, (((0,), (0,)), ((), ())), precision=HIGHEST, preferred_element_type=F32
    ) * (1.0 / subjects)
    col = lax.axis_index("col")
    rows = out_ref.shape[0] - PAD
    out_ref[:rows, :] = full[pl.ds(pl.multiple_of(col * rows, rows), rows), :]
    out_ref[rows:, :] = jnp.zeros((PAD, cols), F32)
    for k in range(mean_ref.shape[1] // cols):
        out_ref[rows + k : rows + k + 1, :] = mean_ref[:, k * cols : (k + 1) * cols]
    own_ref[...] = kept_ref[col] + got_ref[col]


def pair_kernel(copies, mine_ref, got_ref, out_ref, means_ref):
    rows = mine_ref.shape[0] - PAD
    cols = mine_ref.shape[1]
    total = mine_ref[:rows, :] + got_ref[:rows, :]
    for k in range(copies):
        out_ref[k * rows : (k + 1) * rows, :] = total
    for n, ref in enumerate((mine_ref, got_ref)):
        for k in range(means_ref.shape[1] // cols):
            row = ref[rows + k : rows + k + 1, :]
            means_ref[n : n + 1, k * cols : (k + 1) * cols] = row


def cholesky_kernel(block, cross_ref, own_ref, factor_ref, basis_ref, work):
    size = cross_ref.shape[0]
    mine = own_ref.shape[0]
    work[:, :size] = cross_ref[...]
    padded = jnp.concatenate([own_ref[...], jnp.zeros((128 - mine, size), F32)], axis=0)
    work[:, size:] = padded.T
    shape = (block, 128)
    row_id = lax.broadcasted_iota(jnp.int32, shape, 0)

    def spread(value):
        return jnp.broadcast_to(value, shape)

    for start in range(0, size, block):
        lane0 = start // 128 * 128
        chunks = [work[start : start + block, k : k + 128] for k in range(lane0, size + 128, 128)]
        first = start - lane0
        columns = [spread(chunks[0][:, first + j : first + j + 1]) for j in range(block)]
        scale = jnp.zeros(shape, F32)
        for i in range(block):
            pivot = spread(columns[i][i : i + 1, :])
            scale = jnp.where(row_id == i, lax.rsqrt(pivot), scale)
            if i < block - 1:
                weight = jnp.where(row_id > i, columns[i] * (1.0 / pivot), 0.0)
                for j in range(i + 1, block):
                    columns[j] = columns[j] - weight * spread(columns[j][i : i + 1, :])
                chunks = [c - weight * spread(c[i : i + 1, :]) for c in chunks]
        panel = jnp.concatenate([c * scale for c in chunks], axis=1)
        work[start : start + block, lane0:] = panel
        stop = start + block
        if stop < size:
            lane1 = stop // 128 * 128
            right = split_terms(panel[:, lane1 - lane0 :])
            left = [part[:, : size - lane1] for part in right]
            update = lax.dot_general(
                jnp.concatenate([left[k] for k in (0, 0, 1, 0, 2, 1)], axis=0),
                jnp.concatenate([right[k] for k in (0, 1, 0, 2, 0, 1)], axis=0),
                (((0,), (0,)), ((), ())),
                preferred_element_type=F32,
            )
            work[stop:, lane1:] = work[stop:, lane1:] - update[stop - lane1 :, :]
    square = (size, size)
    upper = lax.broadcasted_iota(jnp.int32, square, 0) <= lax.broadcasted_iota(jnp.int32, square, 1)
    factor_ref[...] = jnp.where(upper, work[:, :size], 0.0)
    basis_ref[...] = work[:, size:].T[:mine, :]


def gram_kernel(vox_total, own_ref, other_ref, col_own_ref, col_other_ref, means_ref, _, out_ref, done_ref, cols):
    half = own_ref.shape[1]

    @pl.when(pl.program_id(0) == 0)
    def _():
        for k, ref in enumerate((col_own_ref, col_other_ref)):
            mean = means_ref[k : k + 1, :]
            cols[:, k * half : (k + 1) * half] = (ref[...].astype(F32) - mean).astype(BF16)

    contract = (((1,), (1,)), ((), ()))
    tile = lax.dot_general(own_ref[...], cols[:, :half], contract, preferred_element_type=F32)
    tile += lax.dot_general(other_ref[...], cols[:, half:], contract, preferred_element_type=F32)
    tile = tile * (1.0 / vox_total)
    done_ref[...] = jnp.zeros(done_ref.shape, F32)
    rows = tile.shape[0]
    groups = tile.shape[1] // 128
    for a in range(groups):
        out_ref[pl.ds(a, rows, stride=groups), :] = tile[:, a * 128 : (a + 1) * 128]


def gram_part(vox_total, groups, part, before, own, other, col_own, col_other, means):
    rows, vox_half = own.shape
    tall = min(512, rows // 2)
    steps = rows // tall // 2
    row_spec = pl.BlockSpec((tall, vox_half), lambda i: (i + part * steps, 0))
    col_spec = pl.BlockSpec(col_own.shape, lambda i: (0, 0))
    return pl.pallas_call(
        functools.partial(gram_kernel, vox_total),
        grid=(steps,),
        in_specs=[
            row_spec,
            row_spec,
            col_spec,
            col_spec,
            pl.BlockSpec(means.shape, lambda i: (0, 0)),
            pl.BlockSpec(memory_space=pl.ANY),
        ],
        out_specs=[
            pl.BlockSpec((tall * groups, 128), lambda i: (i + part * steps, 0)),
            pl.BlockSpec((8, 128), lambda i: (0, 0)),
        ],
        out_shape=[sd((rows * groups, 128)), sd((8, 128))],
        scratch_shapes=[pltpu.VMEM((col_own.shape[0], vox_total), BF16)],
        input_output_aliases={} if before is None else {5: 0},
        compiler_params=LARGE,
    )(own, other, col_own, col_other, means, means if before is None else before)


def ring_step(up, down, axis, size, hops=1):
    ahead = [(i, (i + hops) % size) for i in range(size)]
    back = [(i, (i - hops) % size) for i in range(size)]
    return lax.ppermute(up, axis, ahead), lax.ppermute(down, axis, back)


def shards(maps, probes):
    sub_rows, vox_half = maps.shape
    width = probes.shape[1]
    row_count = lax.axis_size("row")
    col_count = lax.axis_size("col")
    vox_count = lax.axis_size("vox")
    subjects = sub_rows * row_count * col_count
    vox_total = vox_half * vox_count
    block_rows = sub_rows * col_count
    groups = row_count // vox_count
    swap = [(0, 1), (1, 0)]

    def exchange(value, axis):
        return lax.all_to_all(value, axis, 0, 0, tiled=True)

    row_maps = lax.all_gather(maps, "col", axis=0, tiled=True)
    slice_rows = vox_half // col_count + PAD
    up1, down1 = ring_step(maps, maps, "row", row_count)
    up2, down2 = ring_step(up1, down1, "row", row_count)
    (local,) = call(
        functools.partial(project_kernel, col_count),
        [sd((col_count * slice_rows, width))],
        maps,
        probes,
        in_specs=[pl.BlockSpec(memory_space=pl.ANY)] * 2,
        params=ALL,
        scratch_shapes=[
            pltpu.VMEM(maps.shape, BF16),
            pltpu.VMEM(probes.shape, BF16),
            pltpu.SemaphoreType.DMA((2,)),
        ],
    )
    (part,) = call(
        functools.partial(sum_repeat_kernel, col_count, row_count),
        [sd((row_count * slice_rows, width))],
        exchange(local, "col"),
        after=[up1, down1, up2, down2],
    )
    half_block = sub_rows // 2
    whole, up2, down2 = call(
        functools.partial(centre_kernel, row_count, col_count, subjects),
        [sd((col_count * slice_rows, width))],
        exchange(part, "row"),
        carry=[up2, down2],
    )
    weights = exchange(whole, "col")
    up3, down3 = ring_step(up2, down2, "row", row_count)
    up4, down4 = ring_step(up2[:half_block], down2[half_block:], "row", row_count, 2)
    ring = [maps, up1, down1, up2, down2, up3, down3, up4, down4]
    places = [(k, 0, sub_rows, shift, 0) for k, shift in enumerate((0, -1, 1, -2, 2, -3, 3))]
    places += [(7, 0, half_block, -4, 0), (8, 0, half_block, 4, half_block)]
    group_shape = (groups, sub_rows, vox_half)
    whole_block = pl.BlockSpec(group_shape, lambda i: (0, 0, 0))
    col_kept, col_sent, sorted_blocks = pl.pallas_call(
        functools.partial(sort_kernel, places),
        grid=(1,),
        in_specs=[pl.BlockSpec(piece.shape, lambda i: (0, 0)) for piece in ring],
        out_specs=[whole_block, whole_block, pl.BlockSpec((8, 128), lambda i: (0, 0))],
        out_shape=[sd(group_shape, BF16), sd(group_shape, BF16), sd((8, 128))],
        compiler_params=SORT,
    )(*ring)

    half_rows = sub_rows // vox_count
    step = min(4 * sub_rows, block_rows)
    half_spec = pl.BlockSpec((step // sub_rows, half_rows, width), lambda i: (i, 0, 0))
    kept, sent, mean, centered = pl.pallas_call(
        functools.partial(sketch_kernel, col_count, vox_total),
        grid=(block_rows // step,),
        in_specs=[
            pl.BlockSpec((step, vox_half), lambda i: (i, 0)),
            pl.BlockSpec((col_count * slice_rows, width), lambda i: (0, 0)),
            pl.BlockSpec(memory_space=pl.ANY),
        ],
        out_specs=[
            half_spec,
            half_spec,
            pl.BlockSpec((1, vox_half), lambda i: (0, 0)),
            pl.BlockSpec((step, vox_half), lambda i: (i, 0)),
        ],
        scratch_shapes=[pltpu.VMEM((2, vox_half, width), BF16)],
        out_shape=[
            sd((col_count, half_rows, width)),
            sd((col_count, half_rows, width)),
            sd((1, vox_half)),
            sd((block_rows, vox_half), BF16),
        ],
        compiler_params=LARGE,
    )(row_maps, weights, sorted_blocks)
    got = lax.ppermute(sent, "vox", swap)
    cross_rows = width // col_count
    slice_shape = (cross_rows + PAD, width)
    slices, own = pl.pallas_call(
        functools.partial(cross_kernel, subjects),
        grid=(1,),
        in_specs=[
            pl.BlockSpec((col_count, half_rows, width), lambda i: (0, 0, 0)),
            pl.BlockSpec((col_count, half_rows, width), lambda i: (0, 0, 0)),
            pl.BlockSpec((1, vox_half), lambda i: (0, 0)),
        ],
        out_specs=[
            pl.BlockSpec(slice_shape, lambda i: (0, 0)),
            pl.BlockSpec((half_rows, width), lambda i: (0, 0)),
        ],
        scratch_shapes=[pltpu.VMEM((width, width), F32)],
        out_shape=[
            sd(slice_shape),
            sd((half_rows, width)),
        ],
        compiler_params=LARGE,
    )(kept, got, mean)
    shared, means, centered, col_sent = call(
        functools.partial(pair_kernel, row_count),
        [sd((row_count * cross_rows, width)), sd((vox_count, vox_half))],
        slices,
        lax.ppermute(slices, "vox", swap),
        carry=[centered, col_sent],
        params=LARGE,
    )

    other = lax.ppermute(centered, "vox", swap)
    col_other = lax.ppermute(col_sent, "vox", swap)
    own_cols = groups * sub_rows
    flat = (own_cols, vox_half)
    operands = (centered, other, col_kept.reshape(flat), col_other.reshape(flat), means)
    gram, first = gram_part(vox_total, groups, 0, None, *operands)
    (summed,) = call(
        functools.partial(sum_repeat_kernel, row_count, col_count),
        [sd((width, width))],
        exchange(shared, "row"),
        after=[first],
    )
    cross = exchange(summed, "col")
    gram, second = gram_part(vox_total, groups, 1, gram, *operands)
    factor, basis = call(
        functools.partial(cholesky_kernel, 16),
        [sd((width, width)), sd((half_rows, width))],
        cross,
        own,
        after=[second],
        scratch_shapes=[pltpu.VMEM((width, width + 128), F32)],
    )
    return gram.reshape(block_rows, groups, 1, sub_rows), basis, factor


def solution(mesh):
    placed = (P(("row", "col"), "vox"), P(("row", "col"), None))
    return jax.shard_map(
        shards,
        mesh=mesh,
        in_specs=placed,
        out_specs=(P("row", "vox", "col", None), P(("row", "col", "vox"), None), P()),
        check_vma=False,
    )
```
